512 devices in a mesh: section: 32 (over y, x, core), dp: 16 (over z).
Axes of the slice: x: 4, y: 4, z: 16, core: 2. Of those that a mesh axis runs over, the one named last changes fastest.
Arguments:
- activations: bfloat16 [32, 2048, 8192], P('section', 'dp'), may hold values from -6 to 6
- norm_gain: float32 [32, 8192], P('section'), may hold values from 0.25 to 1.75
- adapter_down: bfloat16 [32, 8192, 64], P('section', 'dp'), may hold values from -0.0625 to 0.0625
- adapter_up: bfloat16 [32, 8192, 64], P('section', 'dp'), may hold values from -0.0625 to 0.0625
- counts: int32 [16, 4], P('dp'), may hold values from 1 to 32, 96 in all within a row
- upstream: bfloat16 [1536, 8192], P('dp'), may hold values from -6 to 6
Outputs:
- input_grad: bfloat16 [1536, 8192], P('dp', 'section')
- grad_down: float32 [32, 8192, 64], P('section', 'dp')
- grad_up: float32 [32, 8192, 64], P('section', 'dp')
The draws below stay inside these ranges and needn't reach their ends.
Inputs may be any that keep to these rules, and one draw needn't show every extreme that they name: Each replica's 4 counts sum to 96, and the largest of them is 32.
All inputs are finite; a program needn't handle non-finite values.
Results may differ from the reference program's by a relative error of at most 0.04.
Values may be sent and summed in bfloat16 or wider, within the bound.
A program may use at most 64 MiB of HBM per device.

```python
import math
from functools import partial
import jax
import jax.numpy as jnp
import numpy as np
from jax import lax

D = 8192
R = 64
MB = 4
CAP = 32
LIVE = 96
TOKENS = 2048
EVENTS = 1536
N_SECTION = 32
N_DP = 16


def steps_of(key, dims, shards, smallest, top_value):
    factor_of = 1.0
    for dim, blocks in shards:
        draws = jax.random.uniform(jax.random.fold_in(jax.random.fold_in(key, 6), dim), (blocks,), jnp.float32, smallest / len(shards), top_value / len(shards))
        factor_of = factor_of * jnp.repeat(jnp.exp(draws), dims[dim] // blocks).reshape((-1,) + (1,) * (len(dims) - 1 - dim))
    return factor_of


def profile(amount, total, reach, skew):
    portions = [(1 << 20) // math.isqrt(rank ** skew) + 1 for rank in range(2, amount + 1)]
    surplus, given = total - reach - (amount - 1), [1] * (amount - 1)
    while surplus > 0:
        movable = [i for i in range(amount - 1) if given[i] < reach]
        whole, budget = sum([portions[i] for i in movable]), surplus
        for i in movable:
            extra = min(reach - given[i], max(1, budget * portions[i] // whole), surplus)
            given[i] = given[i] + extra
            surplus = surplus - extra
    return np.array([reach] + given)


def uneven(own_key, number_of, total, most, lean):
    if number_of == 2:
        one = jax.random.randint(own_key, (), max(1, total - most), min(most, total - 1) + 1)
        return jnp.stack([one, total - one])
    lengths = jnp.asarray(profile(number_of, total, most, lean), jnp.int32)
    couples = (number_of - 1) // 2
    source_of, sink = lengths[1:1 + 2 * couples:2], lengths[2:2 + 2 * couples:2]
    margin = jnp.minimum(source_of - 1, most - sink)
    passed = jax.random.randint(jax.random.fold_in(own_key, 1), (couples,), 0, 1 << 20) % (margin + 1)
    lengths = lengths.at[1:1 + 2 * couples:2].set(source_of - passed).at[2:2 + 2 * couples:2].set(sink + passed)
    return lengths[jax.random.permutation(jax.random.fold_in(own_key, 2), number_of)]


def scatter_about(key, dims, scale, most, split=(), kind=jnp.bfloat16):
    array = jax.random.normal(key, dims, jnp.float32) * scale
    if len(split) > 0:
        array = steps_of(key, dims, split, -0.22, 0.18) * array
    return jnp.clip(array, min=-most, max=most).astype(kind)


def setup_inputs(seed: int = 0) -> dict:
    streams_of = jax.random.split(jax.random.key(seed), 7)
    activations = scatter_about(streams_of[0], (N_SECTION, TOKENS, D), 1.0, 6.0, ((0, 32), (1, 16)))
    norm_gain = jnp.clip(1.0 + 0.15 * jax.random.normal(streams_of[1], (N_SECTION, D), jnp.float32), 0.25, 1.75)
    adapter_down = scatter_about(streams_of[2], (N_SECTION, D, R), D ** -0.5, 0.0625, ((0, 32), (1, 16)))
    adapter_up = scatter_about(streams_of[3], (N_SECTION, D, R), D ** -0.5, 0.0625, ((0, 32), (1, 16)))
    counts = jax.vmap(lambda own: uneven(own, MB, LIVE, CAP, 2))(jax.random.split(streams_of[4], N_DP)).reshape((N_DP, MB)).astype(jnp.int32)
    upstream = scatter_about(streams_of[5], (EVENTS, D), 1.0, 6.0, ((0, 16),))
    return {"activations": activations, "norm_gain": norm_gain, "adapter_down": adapter_down, "adapter_up": adapter_up, "counts": counts, "upstream": upstream}


ALPHA = 2.0
EPS = 1e-05

def packed_rows(events, live_rows, cap_rows):
    bounds = jnp.cumsum(events, dtype=jnp.int32)
    starts = bounds - events
    position = jnp.arange(live_rows, dtype=jnp.int32)
    member = lax.optimization_barrier(jnp.sum((position[:, None] >= bounds[None, :]).astype(jnp.int32), axis=1, dtype=jnp.int32))
    choose = member[:, None] == jnp.arange(events.shape[0], dtype=jnp.int32)[None, :]
    first_row = lax.optimization_barrier(jnp.sum(jnp.where(choose, starts[None, :], 0), axis=1, dtype=jnp.int32))
    return (member * cap_rows + position - first_row).astype(jnp.int32)

def section_backward(inputs, gain_vector, adapter_lower, adapter_upper, gradient):
    values = inputs.astype(jnp.float32)
    inverse_rms = lax.rsqrt(lax.optimization_barrier(jnp.mean(values * values, axis=-1, keepdims=True)) + EPS)
    scaled = values * inverse_rms
    normed = (scaled * gain_vector).astype(jnp.bfloat16)
    lowered = (ALPHA * jnp.dot(gradient, adapter_upper, preferred_element_type=jnp.float32)).astype(jnp.bfloat16)
    back_norm = lax.dot_general(lowered, adapter_lower, (((1,), (1,)), ((), ())), preferred_element_type=jnp.float32)
    weighted = back_norm * gain_vector
    inner_term = lax.optimization_barrier(jnp.mean(weighted * scaled, axis=-1, keepdims=True))
    next_gradient = (gradient.astype(jnp.float32) + inverse_rms * (weighted - scaled * inner_term)).astype(jnp.bfloat16)
    return (next_gradient, normed, lowered)

def reference(activations, norm_gain, adapter_down, adapter_up, counts, upstream):
    row_index = jax.vmap(partial(packed_rows, live_rows=LIVE, cap_rows=CAP))(counts)
    offsets = (jnp.arange(counts.shape[0], dtype=jnp.int32) * (MB * CAP))[:, None]
    flat_rows = (row_index + offsets).reshape(-1).astype(jnp.int32)
    gradient = upstream
    downs = []
    uppers = []
    for layer_index in range(N_SECTION - 1, -1, -1):
        inputs = jnp.take(activations[layer_index], flat_rows, axis=0)
        next_gradient, normed, lowered = section_backward(inputs, norm_gain[layer_index], adapter_down[layer_index], adapter_up[layer_index], gradient)
        projected = jnp.dot(normed, adapter_down[layer_index], preferred_element_type=jnp.float32).astype(jnp.bfloat16)
        grad_up_layer = ALPHA * lax.dot_general(gradient, projected, (((0,), (0,)), ((), ())), preferred_element_type=jnp.float32) / LIVE
        grad_down_layer = lax.dot_general(normed, lowered, (((0,), (0,)), ((), ())), preferred_element_type=jnp.float32) / LIVE
        downs.append(grad_down_layer)
        uppers.append(grad_up_layer)
        gradient = next_gradient
    grad_down = jnp.stack(downs[::-1], axis=0)
    grad_up = jnp.stack(uppers[::-1], axis=0)
    return (gradient, grad_down, grad_up)
```

```python
import functools

import jax
import jax.numpy as jnp
from jax import lax
from jax.experimental import pallas as pl
from jax.experimental.pallas import tpu as pltpu
from jax.sharding import PartitionSpec as P

ALPHA = 2.0
EPS = 1e-05
QUARTERS = 4
TILE = 16
ROWS = TILE // QUARTERS
MESH = pl.DeviceIdType.MESH
F32 = jnp.float32
BF16 = jnp.bfloat16


def iota(shape, dim):
    return lax.broadcasted_iota(jnp.int32, shape, dim)


def quarter_mask(shape, rank):
    quarter = (iota(shape, 0) // ROWS) % QUARTERS
    return quarter == iota(shape, 1) // rank


def dot(a, b, dims=((1,), (0,)), **kw):
    return lax.dot_general(a, b, (dims, ((), ())), preferred_element_type=F32, **kw)


def kernel(
    n_sec, n_dp, cap,
    counts_ref, x_hbm, gain_ref, down_ref, up_ref, upstream_hbm,
    input_grad_ref, grad_down_ref, grad_up_ref,
    raw, nat, landed, pieces, weight_up, weight_down, held_x, row_scale, coef_rank, projected_all,
    gin, gout, lowered_all, part_up, part_down, slots,
    load_sem, gather_send, gather_recv, chain_send, chain_recv, final_send, final_recv, ring_send, ring_recv,
):
    sec, me = lax.axis_index("section"), lax.axis_index("dp")
    right, left = lax.rem(me + 1, n_dp), lax.rem(me + n_dp - 1, n_dp)
    live, width = nat.shape
    blocks = live // ROWS
    packed = blocks * TILE
    span = width // QUARTERS
    shard, rank = down_ref.shape[1], down_ref.shape[2]
    per_quarter = span // shard
    columns = width // n_sec
    wide = QUARTERS * rank

    load_x = pltpu.make_async_copy(x_hbm.at[0], raw, load_sem.at[0])
    load_x.start()
    load_up = pltpu.make_async_copy(upstream_hbm, nat, load_sem.at[1])

    @pl.when(sec == n_sec - 1)
    def _():
        load_up.start()

    barrier = pltpu.get_barrier_semaphore()
    for side in (left, right):
        pl.semaphore_signal(barrier, inc=1, device_id={"dp": side}, device_id_type=MESH)

    @pl.when(sec > 0)
    def _():
        pl.semaphore_signal(barrier, inc=1, device_id={"section": sec - 1}, device_id_type=MESH)

    @pl.when(sec < n_sec - 1)
    def _():
        pl.semaphore_signal(barrier, inc=1, device_id={"section": sec + 1}, device_id_type=MESH)

    @pl.when(sec > 1)
    def _():
        pl.semaphore_signal(barrier, inc=1, device_id={"section": 0}, device_id_type=MESH)

    @pl.when(sec == 0)
    def _():
        @pl.loop(2, n_sec)
        def _(c):
            pl.semaphore_signal(barrier, inc=1, device_id={"section": c}, device_id_type=MESH)

    my_gain = gain_ref[:, pl.ds(pl.multiple_of(me * shard, shard), shard)]
    pieces[me, 0:rank, :] = up_ref[0].astype(F32).T.astype(BF16)
    pieces[me, rank:2 * rank, :] = (down_ref[0].astype(F32).T * my_gain).astype(BF16)

    @pl.when(sec == 0)
    def _():
        pl.semaphore_wait(barrier, 3 + n_sec - 2)

    @pl.when(sec == 1)
    def _():
        pl.semaphore_wait(barrier, 4)

    @pl.when((sec > 1) & (sec < n_sec - 1))
    def _():
        pl.semaphore_wait(barrier, 5)

    @pl.when(sec == n_sec - 1)
    def _():
        pl.semaphore_wait(barrier, 4)

    def gather_copy(slot, half, way):
        part = pieces.at[slot, pl.ds(half * rank, rank)]
        return pltpu.make_async_remote_copy(
            src_ref=part,
            dst_ref=part,
            send_sem=gather_send.at[way, half, slot],
            recv_sem=gather_recv.at[half, slot],
            device_id={"dp": right if way == 0 else left},
            device_id_type=MESH,
        )

    far = n_dp // 2
    reach = {(0, 0): far, (0, 1): far - 1, (1, 0): far - 1, (1, 1): far}
    for half in (0, 1):
        for way in (0, 1):
            gather_copy(me, half, way).start()

    load_x.wait()
    raw_rows = raw.shape[0]
    prep_rows = raw_rows // far
    scales = []
    for hop in range(1, far + 1):
        for half in (0, 1):
            for way in (0, 1):
                if hop <= reach[way, half]:
                    slot = lax.rem(me + (n_dp - hop if way == 0 else hop), n_dp)
                    here = gather_copy(slot, half, way)
                    here.wait_recv()
                    if hop < reach[way, half]:
                        here.start()
        rows = pl.ds((hop - 1) * prep_rows, prep_rows)
        values = raw[rows, :].astype(F32)
        inverse = lax.rsqrt(jnp.mean(values * values, axis=-1, keepdims=True) + EPS)
        raw[rows, :] = (values * inverse).astype(BF16)
        scales.append(inverse)
    inverse_all = jnp.broadcast_to(jnp.concatenate(scales, axis=0), (raw_rows, 128))

    line = iota((packed, raw_rows), 0)
    position = (line // TILE) * ROWS + lax.rem(line, ROWS)
    source = position
    bound = jnp.int32(0)
    members = counts_ref.shape[1]
    for member in range(members - 1):
        count = counts_ref[0, member]
        bound = bound + count
        source = source + jnp.where(position >= bound, cap - count, 0)
    chosen = source == iota((packed, raw_rows), 1)
    row_scale[...] = dot(chosen.astype(F32), inverse_all, precision=lax.Precision.HIGHEST).reshape(
        blocks, TILE, 128
    )
    quarter = (line // ROWS) % QUARTERS
    picks = [(chosen & (quarter == q)).astype(BF16) for q in range(QUARTERS)]
    for n in range(per_quarter):
        cols = slice(n * shard, (n + 1) * shard)
        total = jnp.zeros((packed, shard), F32)
        for q in range(QUARTERS):
            total += dot(picks[q], raw[:, q * span + n * shard:q * span + (n + 1) * shard])
        held_x[:, :, cols] = total.astype(BF16).reshape(blocks, TILE, shard)

    @pl.when(sec == n_sec - 1)
    def _():
        load_up.wait()
        line = iota((packed, live), 0)
        position = (line // TILE) * ROWS + lax.rem(line, ROWS)
        chosen = position == iota((packed, live), 1)
        quarter = (line // ROWS) % QUARTERS
        for n in range(per_quarter):
            cols = slice(n * shard, (n + 1) * shard)
            total = jnp.zeros((packed, shard), F32)
            for q in range(QUARTERS):
                pick = (chosen & (quarter == q)).astype(BF16)
                total += dot(pick, nat[:, q * span + n * shard:q * span + (n + 1) * shard])
            gin[:, :, cols] = total.astype(BF16).reshape(blocks, TILE, shard)

    for n in range(per_quarter):
        cols = slice(n * shard, (n + 1) * shard)
        stack = jnp.concatenate([pieces[q * per_quarter + n, 0:rank, :] for q in range(QUARTERS)], axis=0)
        weight_up[cols, :] = stack.astype(F32).T.astype(BF16)
        for q in range(QUARTERS):
            weight_down[q * rank:(q + 1) * rank, cols] = pieces[q * per_quarter + n, rank:2 * rank, :]

    def fold(product):
        pair = product[:, 0:128] + product[:, 128:256]
        return pair + pltpu.roll(pair, 64, 1)

    product = dot(held_x[...].reshape(packed, span), weight_down[...], ((1,), (1,)))
    product = jnp.where(quarter_mask((packed, wide), rank), product, 0.0)
    folded = fold(product).reshape(blocks, TILE, 128)
    folded = folded[:, 0:8, :] + folded[:, 8:16, :]
    folded = (folded + pltpu.roll(folded, 4, 1)).astype(BF16).astype(F32)
    lane = lax.broadcasted_iota(jnp.int32, folded.shape, 2)
    coef_rank[...] = jnp.where(lane < rank, folded * (1.0 / width), 0.0)
    tall = jnp.concatenate([folded, folded], axis=1)
    tall = jnp.concatenate([tall, tall], axis=2).reshape(packed, wide)
    projected_all[...] = jnp.where(quarter_mask((packed, wide), rank), tall, 0.0).astype(BF16)

    def chain_copy(block):
        return pltpu.make_async_remote_copy(
            src_ref=gout.at[block],
            dst_ref=gin.at[block],
            send_sem=chain_send.at[block],
            recv_sem=chain_recv.at[block],
            device_id={"section": sec - 1},
            device_id_type=MESH,
        )

    group = 32
    group_blocks = group // ROWS

    def final_copy(k, c):
        rows = pl.ds(pl.multiple_of(k * group, group), group)
        return pltpu.make_async_remote_copy(
            src_ref=nat.at[rows, pl.ds(pl.multiple_of(c * columns, columns), columns)],
            dst_ref=landed.at[rows],
            send_sem=final_send.at[k, c],
            recv_sem=final_recv.at[k],
            device_id={"section": c},
            device_id_type=MESH,
        )

    mask = quarter_mask((TILE, wide), rank)

    def spread(rows8):
        tall = jnp.concatenate([rows8, rows8], axis=0)
        tall = jnp.concatenate([tall, tall], axis=1)
        return jnp.where(mask, tall, 0.0).astype(BF16)

    @pl.loop(0, blocks)
    def _(block):
        @pl.when(sec < n_sec - 1)
        def _():
            pltpu.make_async_remote_copy(
                src_ref=gout.at[block],
                dst_ref=gin.at[block],
                send_sem=chain_send.at[block],
                recv_sem=chain_recv.at[block],
                device_id={"section": lax.rem(sec + n_sec - 1, n_sec)},
                device_id_type=MESH,
            ).wait_recv()

        product = jnp.where(mask, dot(gin[block], weight_up[...]), 0.0)
        pair = fold(product)
        pair = pair[0:8, :] + pair[8:16, :]
        lowered = ((pair + pltpu.roll(pair, 4, 0)) * ALPHA).astype(BF16).astype(F32)
        scaled = lowered * row_scale[block, 0:8, :]
        coef = jnp.sum(scaled * coef_rank[block], axis=-1, keepdims=True)
        coef = jnp.concatenate([coef, coef], axis=0)
        scaled = spread(scaled)
        for n in range(per_quarter):
            cols = slice(n * shard, (n + 1) * shard)
            back = dot(scaled, weight_down[:, cols])
            fresh = gin[block, :, cols].astype(F32) + (back - held_x[block, :, cols].astype(F32) * coef)
            gout[block, :, cols] = fresh.astype(BF16)

        @pl.when(sec > 0)
        def _():
            chain_copy(block).start()

        lowered_all[block] = spread(lowered)

        @pl.when((sec == 0) & (lax.rem(block, group_blocks) == group_blocks - 1))
        def _():
            k = block // group_blocks
            done = gout[pl.ds(k * group_blocks, group_blocks)].reshape(group_blocks * TILE, span)
            shape = (group, group_blocks * TILE)
            row = iota(shape, 0)
            for q in range(QUARTERS):
                want = (row // ROWS) * TILE + q * ROWS + lax.rem(row, ROWS)
                pick = (want == iota(shape, 1)).astype(BF16)
                rows = pl.ds(pl.multiple_of(k * group, group), group)
                nat[rows, q * span:(q + 1) * span] = dot(pick, done).astype(BF16)

            @pl.loop(1, n_sec)
            def _(c):
                final_copy(k, c).start()

    low_t = lowered_all[...].reshape(packed, wide).astype(F32).T.astype(BF16)
    pro_t = projected_all[...].astype(F32).T.astype(BF16)
    for n in range(per_quarter):
        cols = slice(n * shard, (n + 1) * shard)
        part_up[:, cols] = dot(pro_t, gin[:, :, cols].reshape(packed, shard)) * (ALPHA / live)
        part_down[:, cols] = dot(low_t, held_x[:, :, cols].reshape(packed, shard)) * (1.0 / live)

    half_rank = rank // 2
    parts = (part_up, part_down)

    def own(kind, way, piece):
        start = (piece // per_quarter) * rank + way * half_rank
        rows = pl.ds(pl.multiple_of(start, half_rank), half_rank)
        cols = pl.ds(pl.multiple_of(lax.rem(piece, per_quarter) * shard, shard), shard)
        return parts[kind][rows, cols]

    def ring_copy(kind, way, step):
        return pltpu.make_async_remote_copy(
            src_ref=slots.at[kind, way, step],
            dst_ref=slots.at[kind, way, step + 1],
            send_sem=ring_send.at[kind, way, step],
            recv_sem=ring_recv.at[kind, way, step + 1],
            device_id={"dp": right if way == 0 else left},
            device_id_type=MESH,
        )

    streams = [(kind, way) for kind in (0, 1) for way in (0, 1)]

    def piece_at(way, step):
        if way == 0:
            return lax.rem(me + 2 * n_dp - 1 - step, n_dp)
        return lax.rem(me + 1 + step, n_dp)

    for kind, way in streams:
        slots[kind, way, 0] = own(kind, way, piece_at(way, 0)).astype(BF16)
        ring_copy(kind, way, 0).start()

    @pl.loop(1, n_dp - 1)
    def _(step):
        for kind, way in streams:
            ring_copy(kind, way, step - 1).wait_recv()
            total = slots[kind, way, step].astype(F32) + own(kind, way, piece_at(way, step))
            slots[kind, way, step] = total.astype(BF16)
            ring_copy(kind, way, step).start()

    last = n_dp - 1
    totals = []
    for kind, way in streams:
        ring_copy(kind, way, last - 1).wait_recv()
        totals.append(slots[kind, way, last].astype(F32) + own(kind, way, me))
    grad_up_ref[0] = jnp.concatenate(totals[0:2], axis=0).T
    grad_down_ref[0] = (jnp.concatenate(totals[2:4], axis=0) * my_gain).T

    groups = live // group

    @pl.when(sec == 0)
    def _():
        input_grad_ref[...] = nat[:, 0:columns]

        @pl.loop(0, groups)
        def _(k):
            @pl.loop(1, n_sec)
            def _(c):
                final_copy(k, c).wait_send()

    @pl.when(sec > 0)
    def _():
        @pl.loop(0, groups)
        def _(k):
            final_copy(k, sec).wait_recv()

        input_grad_ref[...] = landed[...]

        @pl.loop(0, blocks)
        def _(block):
            chain_copy(block).wait_send()

    for half in (0, 1):
        for way in (0, 1):
            for hop in range(reach[way, half]):
                slot = lax.rem(me + (n_dp - hop if way == 0 else hop), n_dp)
                gather_copy(slot, half, way).wait_send()

    @pl.loop(0, n_dp - 1)
    def _(step):
        for kind, way in streams:
            ring_copy(kind, way, step).wait_send()


def solution(mesh):
    n_sec, n_dp = mesh.shape["section"], mesh.shape["dp"]

    def body(activations, norm_gain, adapter_down, adapter_up, counts, upstream):
        raw_rows, width = activations.shape[1:]
        shard, rank = adapter_down.shape[1:]
        live = upstream.shape[0]
        cap = raw_rows // counts.shape[1]
        blocks = live // ROWS
        packed = blocks * TILE
        span = width // QUARTERS
        wide = QUARTERS * rank
        columns = width // n_sec
        groups = live // 32
        dma = pltpu.SemaphoreType.DMA
        vmem = pl.BlockSpec(memory_space=pltpu.VMEM)
        hbm = pl.BlockSpec(memory_space=pl.ANY)
        return pl.pallas_call(
            functools.partial(kernel, n_sec, n_dp, cap),
            out_shape=(
                jax.ShapeDtypeStruct((live, columns), BF16),
                jax.ShapeDtypeStruct((1, shard, rank), F32),
                jax.ShapeDtypeStruct((1, shard, rank), F32),
            ),
            in_specs=[pl.BlockSpec(memory_space=pltpu.SMEM), hbm, vmem, vmem, vmem, hbm],
            out_specs=(vmem, vmem, vmem),
            scratch_shapes=[
                pltpu.VMEM((raw_rows, width), BF16),
                pltpu.VMEM((live, width), BF16),
                pltpu.VMEM((live, columns), BF16),
                pltpu.VMEM((n_dp, 2 * rank, shard), BF16),
                pltpu.VMEM((span, wide), BF16),
                pltpu.VMEM((wide, span), BF16),
                pltpu.VMEM((blocks, TILE, span), BF16),
                pltpu.VMEM((blocks, TILE, 128), F32),
                pltpu.VMEM((blocks, 8, 128), F32),
                pltpu.VMEM((packed, wide), BF16),
                pltpu.VMEM((blocks, TILE, span), BF16),
                pltpu.VMEM((blocks, TILE, span), BF16),
                pltpu.VMEM((blocks, TILE, wide), BF16),
                pltpu.VMEM((wide, span), F32),
                pltpu.VMEM((wide, span), F32),
                pltpu.VMEM((2, 2, n_dp, rank // 2, shard), BF16),
                dma((2,)),
                dma((2, 2, n_dp)),
                dma((2, n_dp)),
                dma((blocks,)),
                dma((blocks,)),
                dma((groups, n_sec)),
                dma((groups,)),
                dma((2, 2, n_dp)),
                dma((2, 2, n_dp)),
            ],
            compiler_params=pltpu.CompilerParams(
                collective_id=0, has_side_effects=True, vmem_limit_bytes=48 * 1024 * 1024
            ),
        )(counts, activations, norm_gain, adapter_down, adapter_up, upstream)

    return jax.shard_map(
        body,
        mesh=mesh,
        in_specs=(
            P("section", "dp", None),
            P("section", None),
            P("section", "dp", None),
            P("section", "dp", None),
            P("dp", None),
            P("dp", None),
        ),
        out_specs=(P("dp", "section"), P("section", "dp", None), P("section", "dp", None)),
        check_vma=False,
    )
```

```python
import functools

import jax
import jax.numpy as jnp
from jax import lax
from jax.experimental import pallas as pl
from jax.experimental.pallas import tpu as pltpu
from jax.sharding import PartitionSpec as P

ALPHA = 2.0
EPS = 1e-05
QUARTERS = 4
TILE = 16
ROWS = TILE // QUARTERS
MESH = pl.DeviceIdType.MESH
F32 = jnp.float32
BF16 = jnp.bfloat16


def iota(shape, dim):
    return lax.broadcasted_iota(jnp.int32, shape, dim)


def quarter_mask(shape, rank):
    quarter = (iota(shape, 0) // ROWS) % QUARTERS
    return quarter == iota(shape, 1) // rank


def dot(a, b, dims=((1,), (0,)), **kw):
    return lax.dot_general(a, b, (dims, ((), ())), preferred_element_type=F32, **kw)


def kernel(
    n_sec, n_dp, cap,
    counts_hbm, x_hbm, gain_hbm, down_hbm, up_hbm, upstream_hbm,
    input_grad_ref, grad_down_ref, grad_up_ref,
    counts_ref, gain_ref, own_maps, raw, nat, landed, pieces, weight_up, weight_down, held_x, row_scale, coef_rank, projected_all,
    gin, gout, lowered_all, part_up, part_down, slots,
    load_sem, gather_send, gather_recv, chain_send, chain_recv, final_send, final_recv, ring_send, ring_recv,
):
    sec, me = lax.axis_index("section"), lax.axis_index("dp")
    right, left = lax.rem(me + 1, n_dp), lax.rem(me + n_dp - 1, n_dp)
    live, width = nat.shape
    blocks = live // ROWS
    packed = blocks * TILE
    span = width // QUARTERS
    rank, shard = down_hbm.shape[1:]
    per_quarter = span // shard
    columns = width // n_sec
    wide = QUARTERS * rank

    small = [
        pltpu.make_async_copy(up_hbm, own_maps.at[pl.ds(0, 1)], load_sem.at[2]),
        pltpu.make_async_copy(down_hbm, own_maps.at[pl.ds(1, 1)], load_sem.at[3]),
        pltpu.make_async_copy(gain_hbm, gain_ref, load_sem.at[4]),
        pltpu.make_async_copy(counts_hbm, counts_ref, load_sem.at[5]),
    ]
    for load in small:
        load.start()
    load_x = pltpu.make_async_copy(x_hbm.at[0], raw, load_sem.at[0])
    load_x.start()
    load_up = pltpu.make_async_copy(upstream_hbm, nat, load_sem.at[1])

    @pl.when(sec == n_sec - 1)
    def _():
        load_up.start()

    barrier = pltpu.get_barrier_semaphore()
    for side in (left, right):
        pl.semaphore_signal(barrier, inc=1, device_id={"dp": side}, device_id_type=MESH)

    @pl.when(sec > 0)
    def _():
        pl.semaphore_signal(barrier, inc=1, device_id={"section": sec - 1}, device_id_type=MESH)

    @pl.when(sec < n_sec - 1)
    def _():
        pl.semaphore_signal(barrier, inc=1, device_id={"section": sec + 1}, device_id_type=MESH)

    @pl.when(sec > 1)
    def _():
        pl.semaphore_signal(barrier, inc=1, device_id={"section": 0}, device_id_type=MESH)

    @pl.when(sec == 0)
    def _():
        @pl.loop(2, n_sec)
        def _(c):
            pl.semaphore_signal(barrier, inc=1, device_id={"section": c}, device_id_type=MESH)

    for load in small:
        load.wait()
    my_gain = gain_ref[:, pl.ds(pl.multiple_of(me * shard, shard), shard)]
    pieces[me, 0:rank, :] = own_maps[0]
    pieces[me, rank:2 * rank, :] = (own_maps[1].astype(F32) * my_gain).astype(BF16)

    @pl.when(sec == 0)
    def _():
        pl.semaphore_wait(barrier, 3 + n_sec - 2)

    @pl.when(sec == 1)
    def _():
        pl.semaphore_wait(barrier, 4)

    @pl.when((sec > 1) & (sec < n_sec - 1))
    def _():
        pl.semaphore_wait(barrier, 5)

    @pl.when(sec == n_sec - 1)
    def _():
        pl.semaphore_wait(barrier, 4)

    def gather_copy(slot, half, way):
        part = pieces.at[slot, pl.ds(half * rank, rank)]
        return pltpu.make_async_remote_copy(
            src_ref=part,
            dst_ref=part,
            send_sem=gather_send.at[way, half, slot],
            recv_sem=gather_recv.at[half, slot],
            device_id={"dp": right if way == 0 else left},
            device_id_type=MESH,
        )

    far = n_dp // 2
    reach = {(0, 0): far, (0, 1): far - 1, (1, 0): far - 1, (1, 1): far}
    for half in (0, 1):
        for way in (0, 1):
            gather_copy(me, half, way).start()

    load_x.wait()
    raw_rows = raw.shape[0]
    members = counts_ref.shape[1]

    def place(slot):
        rows = pl.ds(pl.multiple_of((slot // per_quarter) * rank, rank), rank)
        cols = pl.ds(pl.multiple_of(lax.rem(slot, per_quarter) * shard, shard), shard)
        weight_down[rows, cols] = pieces[slot, rank:2 * rank, :]

    def sources(shape):
        line = iota(shape, 0)
        position = (line // TILE) * ROWS + lax.rem(line, ROWS)
        source = position
        bound = jnp.int32(0)
        for member in range(members - 1):
            count = counts_ref[0, member]
            bound = bound + count
            source = source + jnp.where(position >= bound, cap - count, 0)
        return source == iota(shape, 1), (line // ROWS) % QUARTERS

    prep_rows = 16
    norm_jobs = raw_rows // prep_rows
    inverses = []

    def work(job):
        if job < norm_jobs:
            rows = pl.ds(job * prep_rows, prep_rows)
            values = raw[rows, :].astype(F32)
            inverse = lax.rsqrt(jnp.mean(values * values, axis=-1, keepdims=True) + EPS)
            raw[rows, :] = (values * inverse).astype(BF16)
            inverses.append(inverse)
        elif job == norm_jobs:
            chosen, _ = sources((packed, raw_rows))
            inverse_all = jnp.broadcast_to(jnp.concatenate(inverses, axis=0), (raw_rows, 128))
            row_scale[...] = dot(
                chosen.astype(F32), inverse_all, precision=lax.Precision.HIGHEST
            ).reshape(blocks, TILE, 128)
        elif job <= norm_jobs + per_quarter:
            n = job - norm_jobs - 1
            chosen, quarter = sources((packed, raw_rows))
            total = jnp.zeros((packed, shard), F32)
            for q in range(QUARTERS):
                pick = (chosen & (quarter == q)).astype(BF16)
                total += dot(pick, raw[:, q * span + n * shard:q * span + (n + 1) * shard])
            held_x[:, :, n * shard:(n + 1) * shard] = total.astype(BF16).reshape(blocks, TILE, shard)

    jobs = norm_jobs + 1 + per_quarter
    done = 0
    turns = 2 * far
    turn = 0
    place(me)
    for hop in range(1, far + 1):
        for half in (0, 1):
            for way in (0, 1):
                if hop <= reach[way, half]:
                    slot = lax.rem(me + (n_dp - hop if way == 0 else hop), n_dp)
                    here = gather_copy(slot, half, way)
                    here.wait_recv()
                    if hop < reach[way, half]:
                        here.start()
                    if half == 1:
                        place(slot)
            turn += 1
            while done * turns < jobs * turn:
                work(done)
                done += 1

    @pl.when(sec == n_sec - 1)
    def _():
        load_up.wait()
        line = iota((packed, live), 0)
        position = (line // TILE) * ROWS + lax.rem(line, ROWS)
        chosen = position == iota((packed, live), 1)
        quarter = (line // ROWS) % QUARTERS
        for n in range(per_quarter):
            cols = slice(n * shard, (n + 1) * shard)
            total = jnp.zeros((packed, shard), F32)
            for q in range(QUARTERS):
                pick = (chosen & (quarter == q)).astype(BF16)
                total += dot(pick, nat[:, q * span + n * shard:q * span + (n + 1) * shard])
            gin[:, :, cols] = total.astype(BF16).reshape(blocks, TILE, shard)

    for n in range(per_quarter):
        cols = slice(n * shard, (n + 1) * shard)
        stack = jnp.concatenate([pieces[q * per_quarter + n, 0:rank, :] for q in range(QUARTERS)], axis=0)
        weight_up[cols, :] = stack.T

    def fold(product):
        pair = product[:, 0:128] + product[:, 128:256]
        return pair + pltpu.roll(pair, 64, 1)

    product = dot(held_x[...].reshape(packed, span), weight_down[...], ((1,), (1,)))
    product = jnp.where(quarter_mask((packed, wide), rank), product, 0.0)
    folded = fold(product).reshape(blocks, TILE, 128)
    folded = folded[:, 0:8, :] + folded[:, 8:16, :]
    folded = (folded + pltpu.roll(folded, 4, 1)).astype(BF16).astype(F32)
    lane = lax.broadcasted_iota(jnp.int32, folded.shape, 2)
    coef_rank[...] = jnp.where(lane < rank, folded * (1.0 / width), 0.0)
    tall = jnp.concatenate([folded, folded], axis=1)
    tall = jnp.concatenate([tall, tall], axis=2).reshape(packed, wide)
    projected_all[...] = jnp.where(quarter_mask((packed, wide), rank), tall, 0.0).astype(BF16)

    def chain_copy(block):
        return pltpu.make_async_remote_copy(
            src_ref=gout.at[block],
            dst_ref=gin.at[block],
            send_sem=chain_send.at[block],
            recv_sem=chain_recv.at[block],
            device_id={"section": sec - 1},
            device_id_type=MESH,
        )

    group = 32
    group_blocks = group // ROWS

    def final_copy(k, c):
        rows = pl.ds(pl.multiple_of(k * group, group), group)
        return pltpu.make_async_remote_copy(
            src_ref=nat.at[rows, pl.ds(pl.multiple_of(c * columns, columns), columns)],
            dst_ref=landed.at[rows],
            send_sem=final_send.at[k, c],
            recv_sem=final_recv.at[k],
            device_id={"section": c},
            device_id_type=MESH,
        )

    mask = quarter_mask((TILE, wide), rank)

    def spread(rows8):
        tall = jnp.concatenate([rows8, rows8], axis=0)
        tall = jnp.concatenate([tall, tall], axis=1)
        return jnp.where(mask, tall, 0.0).astype(BF16)

    @pl.loop(0, blocks)
    def _(block):
        @pl.when(sec < n_sec - 1)
        def _():
            pltpu.make_async_remote_copy(
                src_ref=gout.at[block],
                dst_ref=gin.at[block],
                send_sem=chain_send.at[block],
                recv_sem=chain_recv.at[block],
                device_id={"section": lax.rem(sec + n_sec - 1, n_sec)},
                device_id_type=MESH,
            ).wait_recv()

        product = jnp.where(mask, dot(gin[block], weight_up[...]), 0.0)
        pair = fold(product)
        pair = pair[0:8, :] + pair[8:16, :]
        lowered = ((pair + pltpu.roll(pair, 4, 0)) * ALPHA).astype(BF16).astype(F32)
        scaled = lowered * row_scale[block, 0:8, :]
        coef = jnp.sum(scaled * coef_rank[block], axis=-1, keepdims=True)
        coef = jnp.concatenate([coef, coef], axis=0)
        scaled = spread(scaled)
        for n in range(per_quarter):
            cols = slice(n * shard, (n + 1) * shard)
            back = dot(scaled, weight_down[:, cols])
            fresh = gin[block, :, cols].astype(F32) + (back - held_x[block, :, cols].astype(F32) * coef)
            gout[block, :, cols] = fresh.astype(BF16)

        @pl.when(sec > 0)
        def _():
            chain_copy(block).start()

        lowered_all[block] = spread(lowered)

        @pl.when((sec == 0) & (lax.rem(block, group_blocks) == group_blocks - 1))
        def _():
            k = block // group_blocks
            done = gout[pl.ds(k * group_blocks, group_blocks)].reshape(group_blocks * TILE, span)
            shape = (group, group_blocks * TILE)
            row = iota(shape, 0)
            for q in range(QUARTERS):
                want = (row // ROWS) * TILE + q * ROWS + lax.rem(row, ROWS)
                pick = (want == iota(shape, 1)).astype(BF16)
                rows = pl.ds(pl.multiple_of(k * group, group), group)
                nat[rows, q * span:(q + 1) * span] = dot(pick, done).astype(BF16)

            @pl.loop(1, n_sec)
            def _(c):
                final_copy(k, c).start()

    low_t = lowered_all[...].reshape(packed, wide).astype(F32).T.astype(BF16)
    pro_t = projected_all[...].astype(F32).T.astype(BF16)
    half_rank = rank // 2
    parts = (part_up, part_down)

    def own(kind, half, piece):
        start = (piece // per_quarter) * rank + half * half_rank
        rows = pl.ds(pl.multiple_of(start, half_rank), half_rank)
        cols = pl.ds(pl.multiple_of(lax.rem(piece, per_quarter) * shard, shard), shard)
        return parts[kind][rows, cols]

    def ring_copy(kind, way, half, step):
        return pltpu.make_async_remote_copy(
            src_ref=slots.at[kind, way, half, step],
            dst_ref=slots.at[kind, way, half, step + 1],
            send_sem=ring_send.at[kind, way, half, step],
            recv_sem=ring_recv.at[kind, way, half, step + 1],
            device_id={"dp": right if way == 0 else left},
            device_id_type=MESH,
        )

    def target(kind, way, step):
        distance = reach[way, kind] - step
        return lax.rem(me + (distance if way == 0 else n_dp - distance), n_dp)

    def partial(offset):
        cols = pl.ds(pl.multiple_of(lax.rem(me + far + per_quarter + offset, per_quarter) * shard, shard), shard)
        part_up[:, cols] = dot(pro_t, gin[:, :, cols].reshape(packed, shard)) * (ALPHA / live)
        part_down[:, cols] = dot(low_t, held_x[:, :, cols].reshape(packed, shard)) * (1.0 / live)

    def begin(kind, way):
        for half in (0, 1):
            slots[kind, way, half, 0] = own(kind, half, target(kind, way, 0)).astype(BF16)
            ring_copy(kind, way, half, 0).start()

    def forward(kind, way, step):
        for half in (0, 1):
            ring_copy(kind, way, half, step - 1).wait_recv()
            total = slots[kind, way, half, step].astype(F32) + own(kind, half, target(kind, way, step))
            slots[kind, way, half, step] = total.astype(BF16)
            ring_copy(kind, way, half, step).start()

    partial(0)
    begin(0, 0)
    begin(1, 1)
    partial(-1)
    begin(1, 0)
    partial(1)
    begin(0, 1)
    partial(2)
    streams = [(0, 0), (1, 1), (1, 0), (0, 1)]

    @pl.loop(1, far - 1)
    def _(step):
        for kind, way in streams:
            forward(kind, way, step)

    for kind, way in streams[0:2]:
        forward(kind, way, far - 1)

    sums = []
    for kind in (0, 1):
        for half in (0, 1):
            total = own(kind, half, me)
            for way in (1 - kind, kind):
                ring_copy(kind, way, half, reach[way, kind] - 1).wait_recv()
                total += slots[kind, way, half, reach[way, kind]].astype(F32)
            sums.append(total)
    for half in (0, 1):
        rows = slice(half * half_rank, (half + 1) * half_rank)
        grad_up_ref[0, rows, :] = sums[half]
        grad_down_ref[0, rows, :] = sums[2 + half] * my_gain

    groups = live // group

    @pl.when(sec == 0)
    def _():
        input_grad_ref[...] = nat[:, 0:columns]

        @pl.loop(0, groups)
        def _(k):
            @pl.loop(1, n_sec)
            def _(c):
                final_copy(k, c).wait_send()

    @pl.when(sec > 0)
    def _():
        @pl.loop(0, groups)
        def _(k):
            final_copy(k, sec).wait_recv()

        input_grad_ref[...] = landed[...]

        @pl.loop(0, blocks)
        def _(block):
            chain_copy(block).wait_send()

    for half in (0, 1):
        for way in (0, 1):
            for hop in range(reach[way, half]):
                slot = lax.rem(me + (n_dp - hop if way == 0 else hop), n_dp)
                gather_copy(slot, half, way).wait_send()

    for kind, way in streams:
        @pl.loop(0, reach[way, kind])
        def _(step):
            for half in (0, 1):
                ring_copy(kind, way, half, step).wait_send()


def solution(mesh):
    n_sec, n_dp = mesh.shape["section"], mesh.shape["dp"]

    def body(activations, norm_gain, adapter_down, adapter_up, counts, upstream):
        raw_rows, width = activations.shape[1:]
        down_t, up_t = jnp.swapaxes(adapter_down, 1, 2), jnp.swapaxes(adapter_up, 1, 2)
        rank, shard = down_t.shape[1:]
        live = upstream.shape[0]
        cap = raw_rows // counts.shape[1]
        blocks = live // ROWS
        packed = blocks * TILE
        span = width // QUARTERS
        wide = QUARTERS * rank
        columns = width // n_sec
        groups = live // 32
        dma = pltpu.SemaphoreType.DMA
        vmem = pl.BlockSpec(memory_space=pltpu.VMEM)
        hbm = pl.BlockSpec(memory_space=pl.ANY)
        input_grad, grad_down, grad_up = pl.pallas_call(
            functools.partial(kernel, n_sec, n_dp, cap),
            out_shape=(
                jax.ShapeDtypeStruct((live, columns), BF16),
                jax.ShapeDtypeStruct((1, rank, shard), F32),
                jax.ShapeDtypeStruct((1, rank, shard), F32),
            ),
            in_specs=[hbm] * 6,
            out_specs=(vmem, vmem, vmem),
            scratch_shapes=[
                pltpu.SMEM(counts.shape, jnp.int32),
                pltpu.VMEM((1, width), F32),
                pltpu.VMEM((2, rank, shard), BF16),
                pltpu.VMEM((raw_rows, width), BF16),
                pltpu.VMEM((live, width), BF16),
                pltpu.VMEM((live, columns), BF16),
                pltpu.VMEM((n_dp, 2 * rank, shard), BF16),
                pltpu.VMEM((span, wide), BF16),
                pltpu.VMEM((wide, span), BF16),
                pltpu.VMEM((blocks, TILE, span), BF16),
                pltpu.VMEM((blocks, TILE, 128), F32),
                pltpu.VMEM((blocks, 8, 128), F32),
                pltpu.VMEM((packed, wide), BF16),
                pltpu.VMEM((blocks, TILE, span), BF16),
                pltpu.VMEM((blocks, TILE, span), BF16),
                pltpu.VMEM((blocks, TILE, wide), BF16),
                pltpu.VMEM((wide, span), F32),
                pltpu.VMEM((wide, span), F32),
                pltpu.VMEM((2, 2, 2, n_dp // 2 + 1, rank // 2, shard), BF16),
                dma((6,)),
                dma((2, 2, n_dp)),
                dma((2, n_dp)),
                dma((blocks,)),
                dma((blocks,)),
                dma((groups, n_sec)),
                dma((groups,)),
                dma((2, 2, 2, n_dp // 2 + 1)),
                dma((2, 2, 2, n_dp // 2 + 1)),
            ],
            compiler_params=pltpu.CompilerParams(
                collective_id=0, has_side_effects=True, vmem_limit_bytes=63 * 1024 * 1024
            ),
        )(counts, activations, norm_gain, down_t, up_t, upstream)
        return input_grad, jnp.swapaxes(grad_down, 1, 2), jnp.swapaxes(grad_up, 1, 2)

    return jax.shard_map(
        body,
        mesh=mesh,
        in_specs=(
            P("section", "dp", None),
            P("section", None),
            P("section", "dp", None),
            P("section", "dp", None),
            P("dp", None),
            P("dp", None),
        ),
        out_specs=(P("dp", "section"), P("section", "dp", None), P("section", "dp", None)),
        check_vma=False,
    )
```

```python
import functools

import jax
import jax.numpy as jnp
from jax import lax
from jax.experimental import pallas as pl
from jax.experimental.pallas import tpu as pltpu
from jax.sharding import PartitionSpec as P

ALPHA = 2.0
EPS = 1e-05
QUARTERS = 4
TILE = 16
ROWS = TILE // QUARTERS
MESH = pl.DeviceIdType.MESH
F32 = jnp.float32
BF16 = jnp.bfloat16


def iota(shape, dim):
    return lax.broadcasted_iota(jnp.int32, shape, dim)


def quarter_mask(shape, rank):
    quarter = (iota(shape, 0) // ROWS) % QUARTERS
    return quarter == iota(shape, 1) // rank


def dot(a, b, dims=((1,), (0,)), **kw):
    return lax.dot_general(a, b, (dims, ((), ())), preferred_element_type=F32, **kw)


def kernel(
    n_sec, n_dp, cap,
    counts_hbm, x_hbm, gain_hbm, down_hbm, up_hbm, upstream_hbm,
    input_grad_ref, grad_down_ref, grad_up_ref,
    counts_ref, gain_ref, own_maps, raw, nat, landed, pieces, weight_up, weight_down,
    held_x, row_scale, other_x, other_scale, coef_rank, projected_all,
    gin, gout, lowered_all, part_up, part_down, lent, borrowed, slots,
    load_sem, gather_send, gather_recv, share_send, share_recv, swap_send, swap_recv,
    chain_send, chain_recv, lend_send, lend_recv, final_send, final_recv, ring_send, ring_recv,
):
    sec, me = lax.axis_index("section"), lax.axis_index("dp")
    right, left = lax.rem(me + 1, n_dp), lax.rem(me + n_dp - 1, n_dp)
    core = lax.rem(sec, 2)
    other = 1 - core
    mate = sec + 1 - 2 * core
    half_rows, width = nat.shape
    live = 2 * half_rows
    blocks = half_rows // ROWS
    packed = blocks * TILE
    span = width // QUARTERS
    rank, shard = down_hbm.shape[1:]
    per_quarter = span // shard
    columns = width // n_sec
    wide = QUARTERS * rank
    far = n_dp // 2
    is_top, is_end = sec >= n_sec - 2, sec < 2

    small = [
        pltpu.make_async_copy(up_hbm, own_maps.at[pl.ds(0, 1)], load_sem.at[2]),
        pltpu.make_async_copy(down_hbm, own_maps.at[pl.ds(1, 1)], load_sem.at[3]),
        pltpu.make_async_copy(gain_hbm, gain_ref, load_sem.at[4]),
        pltpu.make_async_copy(counts_hbm, counts_ref, load_sem.at[5]),
    ]
    for load in small:
        load.start()
    load_x = pltpu.make_async_copy(x_hbm.at[0], raw, load_sem.at[0])
    load_x.start()
    my_half = pl.ds(pl.multiple_of(core * half_rows, half_rows), half_rows)
    load_up = pltpu.make_async_copy(upstream_hbm.at[my_half], nat, load_sem.at[1])

    @pl.when(is_top)
    def _():
        load_up.start()

    barrier = pltpu.get_barrier_semaphore()

    def greet(**where):
        pl.semaphore_signal(barrier, inc=1, device_id=where, device_id_type=MESH)

    greet(dp=left)
    greet(dp=right)
    greet(section=mate)

    @pl.when(sec >= 2)
    def _():
        greet(section=sec - 2)

    @pl.when(sec < n_sec - 2)
    def _():
        greet(section=sec + 2)

    for end in (0, 1):
        @pl.when((sec >= 2) & (sec != end + 2))
        def _():
            greet(section=end)

    @pl.when(is_end)
    def _():
        @pl.loop(2, n_sec)
        def _(c):
            @pl.when(c != sec + 2)
            def _():
                greet(section=c)

    for load in small:
        load.wait()
    my_gain = gain_ref[:, pl.ds(pl.multiple_of(me * shard, shard), shard)]
    pieces[core, me, 0:rank, :] = own_maps[0]
    pieces[core, me, rank:2 * rank, :] = (own_maps[1].astype(F32) * my_gain).astype(BF16)

    def greeted(when, amount):
        @pl.when(when)
        def _():
            pl.semaphore_wait(barrier, amount)

    near_end = (sec >= 2) & (sec < 4)
    greeted(is_end, 3 + 1 + n_sec - 3)
    if n_sec > 4:
        greeted(near_end, 3 + 2 + 1)
        greeted((sec >= 4) & (sec < n_sec - 2), 3 + 2 + 2)
        greeted(is_top, 3 + 1 + 2)
    else:
        greeted(near_end, 3 + 1 + 1)

    def gather_copy(slot, half, way):
        part = pieces.at[core, slot, pl.ds(half * rank, rank)]
        return pltpu.make_async_remote_copy(
            src_ref=part,
            dst_ref=part,
            send_sem=gather_send.at[way, half, slot],
            recv_sem=gather_recv.at[half, slot],
            device_id={"dp": right if way == 0 else left},
            device_id_type=MESH,
        )

    def to_mate(source, target, send_sem, recv_sem):
        return pltpu.make_async_remote_copy(
            src_ref=source,
            dst_ref=target,
            send_sem=send_sem,
            recv_sem=recv_sem,
            device_id={"section": mate},
            device_id_type=MESH,
        )

    def share_copy(parity, slot, half):
        part = pieces.at[parity, slot, pl.ds(half * rank, rank)]
        return to_mate(part, part, share_send.at[half, slot], share_recv.at[half, slot])

    def scale_copy(parity):
        return to_mate(other_scale, row_scale.at[parity], swap_send.at[0], swap_recv.at[0])

    def x_copy(parity):
        return to_mate(other_x, held_x.at[parity], swap_send.at[1], swap_recv.at[1])

    reach = {(0, 0): far, (0, 1): far - 1, (1, 0): far - 1, (1, 1): far}
    for half in (0, 1):
        for way in (0, 1):
            gather_copy(me, half, way).start()
    for half in (0, 1):
        share_copy(core, me, half).start()

    load_x.wait()
    raw_rows = raw.shape[0]
    members = counts_ref.shape[1]

    def place(parity, slot):
        rows = pl.ds(pl.multiple_of((slot // per_quarter) * rank, rank), rank)
        cols = pl.ds(pl.multiple_of(lax.rem(slot, per_quarter) * shard, shard), shard)
        weight_down[parity, rows, cols] = pieces[parity, slot, rank:2 * rank, :]

    def sources(shape, half):
        line = iota(shape, 0)
        position = half * half_rows + (line // TILE) * ROWS + lax.rem(line, ROWS)
        source = position
        bound = jnp.int32(0)
        for member in range(members - 1):
            count = counts_ref[0, member]
            bound = bound + count
            source = source + jnp.where(position >= bound, cap - count, 0)
        return source == iota(shape, 1), (line // ROWS) % QUARTERS

    prep_rows = 16
    norm_jobs = raw_rows // prep_rows
    inverses = []

    def pack(n, half):
        chosen, quarter = sources((packed, raw_rows), half)
        total = jnp.zeros((packed, shard), F32)
        for q in range(QUARTERS):
            pick = (chosen & (quarter == q)).astype(BF16)
            total += dot(pick, raw[:, q * span + n * shard:q * span + (n + 1) * shard])
        return total.astype(BF16).reshape(blocks, TILE, shard)

    def work(job):
        if job < norm_jobs:
            rows = pl.ds(job * prep_rows, prep_rows)
            values = raw[rows, :].astype(F32)
            inverse = lax.rsqrt(jnp.mean(values * values, axis=-1, keepdims=True) + EPS)
            raw[rows, :] = (values * inverse).astype(BF16)
            inverses.append(inverse)
        elif job == norm_jobs:
            inverse_all = jnp.broadcast_to(jnp.concatenate(inverses, axis=0), (raw_rows, 128))
            for half in (other, core):
                chosen, _ = sources((packed, raw_rows), half)
                scale = dot(chosen.astype(F32), inverse_all, precision=lax.Precision.HIGHEST)
                scale = scale.reshape(blocks, TILE, 128)
                if half is other:
                    other_scale[...] = scale
                    scale_copy(core).start()
                else:
                    row_scale[core] = scale
        elif job <= norm_jobs + per_quarter:
            n = job - norm_jobs - 1
            other_x[:, :, n * shard:(n + 1) * shard] = pack(n, other)
            if n == per_quarter - 1:
                x_copy(core).start()
        elif job <= norm_jobs + 2 * per_quarter:
            n = job - norm_jobs - 1 - per_quarter
            held_x[core, :, :, n * shard:(n + 1) * shard] = pack(n, core)

    jobs = norm_jobs + 1 + 2 * per_quarter
    done = 0
    turns = 2 * far
    turn = 0

    def from_mate(hop):
        for slot in [me] if hop == 0 else [lax.rem(me + n_dp - hop, n_dp), lax.rem(me + hop, n_dp)]:
            for half in (0, 1):
                share_copy(other, slot, half).wait_recv()
            place(other, slot)
            if hop == far:
                break

    place(core, me)
    for hop in range(1, far + 1):
        for half in (0, 1):
            for way in (0, 1):
                if hop <= reach[way, half]:
                    slot = lax.rem(me + (n_dp - hop if way == 0 else hop), n_dp)
                    here = gather_copy(slot, half, way)
                    here.wait_recv()
                    if hop < reach[way, half]:
                        here.start()
                    share_copy(core, slot, half).start()
                    if half == 1:
                        place(core, slot)
            turn += 1
            while done * turns < jobs * turn:
                work(done)
                done += 1
        from_mate(hop - 1)

    @pl.when(is_top)
    def _():
        load_up.wait()
        line = iota((packed, half_rows), 0)
        position = (line // TILE) * ROWS + lax.rem(line, ROWS)
        chosen = position == iota((packed, half_rows), 1)
        quarter = (line // ROWS) % QUARTERS
        for n in range(per_quarter):
            cols = slice(n * shard, (n + 1) * shard)
            total = jnp.zeros((packed, shard), F32)
            for q in range(QUARTERS):
                pick = (chosen & (quarter == q)).astype(BF16)
                total += dot(pick, nat[:, q * span + n * shard:q * span + (n + 1) * shard])
            gin[1, :, :, cols] = total.astype(BF16).reshape(blocks, TILE, shard)

    from_mate(far)
    scale_copy(other).wait_recv()
    x_copy(other).wait_recv()

    for parity in (1, 0):
        for n in range(per_quarter):
            stack = [pieces[parity, q * per_quarter + n, 0:rank, :] for q in range(QUARTERS)]
            weight_up[parity, n * shard:(n + 1) * shard, :] = jnp.concatenate(stack, axis=0).T

    def fold(product):
        pair = product[:, 0:128] + product[:, 128:256]
        return pair + pltpu.roll(pair, 64, 1)

    for parity in (1, 0):
        product = dot(held_x[parity].reshape(packed, span), weight_down[parity], ((1,), (1,)))
        product = jnp.where(quarter_mask((packed, wide), rank), product, 0.0)
        folded = fold(product).reshape(blocks, TILE, 128)
        folded = folded[:, 0:8, :] + folded[:, 8:16, :]
        folded = (folded + pltpu.roll(folded, 4, 1)).astype(BF16).astype(F32)
        lane = lax.broadcasted_iota(jnp.int32, folded.shape, 2)
        coef_rank[parity] = jnp.where(lane < rank, folded * (1.0 / width), 0.0)
        tall = jnp.concatenate([folded, folded], axis=1)
        tall = jnp.concatenate([tall, tall], axis=2).reshape(packed, wide)
        projected_all[parity] = jnp.where(quarter_mask((packed, wide), rank), tall, 0.0).astype(BF16)

    def chain_copy(block):
        return pltpu.make_async_remote_copy(
            src_ref=gout.at[block],
            dst_ref=gin.at[1, block],
            send_sem=chain_send.at[block],
            recv_sem=chain_recv.at[block],
            device_id={"section": lax.rem(sec + n_sec - 2, n_sec)},
            device_id_type=MESH,
        )

    group = 16
    group_blocks = group // ROWS
    groups = half_rows // group

    def final_copy(half, k, c):
        rows = pl.ds(pl.multiple_of(k * group, group), group)
        return pltpu.make_async_remote_copy(
            src_ref=nat.at[rows, pl.ds(pl.multiple_of(c * columns, columns), columns)],
            dst_ref=landed.at[pl.ds(pl.multiple_of(half * half_rows + k * group, group), group)],
            send_sem=final_send.at[k, c],
            recv_sem=final_recv.at[half, k],
            device_id={"section": c},
            device_id_type=MESH,
        )

    mask = quarter_mask((TILE, wide), rank)

    def spread(rows8):
        tall = jnp.concatenate([rows8, rows8], axis=0)
        tall = jnp.concatenate([tall, tall], axis=1)
        return jnp.where(mask, tall, 0.0).astype(BF16)

    def unpack(block):
        k = block // group_blocks
        finished = gout[pl.ds(k * group_blocks, group_blocks)].reshape(group_blocks * TILE, span)
        shape = (group, group_blocks * TILE)
        row = iota(shape, 0)
        rows = pl.ds(pl.multiple_of(k * group, group), group)
        for q in range(QUARTERS):
            want = (row // ROWS) * TILE + q * ROWS + lax.rem(row, ROWS)
            pick = (want == iota(shape, 1)).astype(BF16)
            nat[rows, q * span:(q + 1) * span] = dot(pick, finished).astype(BF16)

        @pl.loop(0, n_sec)
        def _(c):
            @pl.when(c != sec)
            def _():
                final_copy(core, k, c).start()

    def layer(parity, block, result):
        values = gin[parity, block]
        product = dot(values, weight_up[parity])
        pair = fold(jnp.where(mask, product, 0.0))
        pair = pair[0:8, :] + pair[8:16, :]
        lowered = ((pair + pltpu.roll(pair, 4, 0)) * ALPHA).astype(BF16).astype(F32)
        scaled = lowered * row_scale[parity, block, 0:8, :]
        coef = jnp.sum(scaled * coef_rank[parity, block], axis=-1, keepdims=True)
        coef = jnp.concatenate([coef, coef], axis=0)
        back = dot(spread(scaled), weight_down[parity])
        fresh = values.astype(F32) + (back - held_x[parity, block].astype(F32) * coef)
        result[...] = fresh.astype(BF16)
        return lowered

    def run_chain(receives, sends):
        @pl.loop(0, blocks)
        def _(block):
            if receives:
                chain_copy(block).wait_recv()
            first = layer(1, block, gin.at[0, block])
            second = layer(0, block, gout.at[block])
            if sends:
                chain_copy(block).start()
            lowered_all[1, block] = spread(first)
            lowered_all[0, block] = spread(second)
            if not sends:
                @pl.when(lax.rem(block, group_blocks) == group_blocks - 1)
                def _():
                    unpack(block)

    @pl.when(is_top)
    def _():
        run_chain(False, True)

    if n_sec > 4:
        @pl.when((sec >= 2) & (sec < n_sec - 2))
        def _():
            run_chain(True, True)

    @pl.when(is_end)
    def _():
        run_chain(True, False)

    half_rank = rank // 2
    parts = (part_up, part_down)
    offsets = (0, -1, 1, 2)[:per_quarter]

    def chunk_at(offset):
        return lax.rem(me + far + per_quarter + offset, per_quarter)

    def flip(values):
        return values.astype(F32).T.astype(BF16)

    def lend_copy(kind, n):
        return to_mate(
            lent.at[kind, n], borrowed.at[kind, n], lend_send.at[kind, n], lend_recv.at[kind, n]
        )

    def products(parity, n):
        cols = pl.ds(pl.multiple_of(n * shard, shard), shard)
        up = dot(flipped[parity is core][0], gin[parity, :, :, cols].reshape(packed, shard))
        down = dot(flipped[parity is core][1], held_x[parity, :, :, cols].reshape(packed, shard))
        return cols, up * (ALPHA / live), down * (1.0 / live)

    flipped = {
        parity is core: (flip(projected_all[parity]), flip(lowered_all[parity].reshape(packed, wide)))
        for parity in (other, core)
    }
    for offset in offsets:
        n = chunk_at(offset)
        _, up, down = products(other, n)
        lent[0, n] = up.astype(BF16)
        lend_copy(0, n).start()
        lent[1, n] = down.astype(BF16)
        lend_copy(1, n).start()

    def partial(offset):
        if offset not in offsets:
            return
        n = chunk_at(offset)
        cols, up, down = products(core, n)
        for kind in (0, 1):
            lend_copy(kind, n).wait_recv()
        part_up[:, cols] = up + borrowed[0, n].astype(F32)
        part_down[:, cols] = down + borrowed[1, n].astype(F32)

    def own(kind, half, piece):
        start = (piece // per_quarter) * rank + half * half_rank
        rows = pl.ds(pl.multiple_of(start, half_rank), half_rank)
        cols = pl.ds(pl.multiple_of(lax.rem(piece, per_quarter) * shard, shard), shard)
        return parts[kind][rows, cols]

    def ring_copy(kind, way, half, step):
        return pltpu.make_async_remote_copy(
            src_ref=slots.at[kind, way, half, step],
            dst_ref=slots.at[kind, way, half, step + 1],
            send_sem=ring_send.at[kind, way, half, step],
            recv_sem=ring_recv.at[kind, way, half, step + 1],
            device_id={"dp": right if way == 0 else left},
            device_id_type=MESH,
        )

    def target(kind, way, step):
        distance = reach[way, kind] - step
        return lax.rem(me + (distance if way == 0 else n_dp - distance), n_dp)

    def begin(kind, way):
        for half in (0, 1):
            slots[kind, way, half, 0] = own(kind, half, target(kind, way, 0)).astype(BF16)
            ring_copy(kind, way, half, 0).start()

    def forward(kind, way, step):
        for half in (0, 1):
            ring_copy(kind, way, half, step - 1).wait_recv()
            total = slots[kind, way, half, step].astype(F32) + own(kind, half, target(kind, way, step))
            slots[kind, way, half, step] = total.astype(BF16)
            ring_copy(kind, way, half, step).start()

    partial(0)
    begin(0, 0)
    begin(1, 1)
    partial(-1)
    begin(1, 0)
    partial(1)
    begin(0, 1)
    partial(2)
    streams = [(0, 0), (1, 1), (1, 0), (0, 1)]

    @pl.loop(1, far - 1)
    def _(step):
        for kind, way in streams:
            forward(kind, way, step)

    for kind, way in streams[0:2]:
        forward(kind, way, far - 1)

    sums = []
    for kind in (0, 1):
        for half in (0, 1):
            total = own(kind, half, me)
            for way in (1 - kind, kind):
                ring_copy(kind, way, half, reach[way, kind] - 1).wait_recv()
                total += slots[kind, way, half, reach[way, kind]].astype(F32)
            sums.append(total)
    for half in (0, 1):
        rows = slice(half * half_rank, (half + 1) * half_rank)
        grad_up_ref[0, rows, :] = sums[half]
        grad_down_ref[0, rows, :] = sums[2 + half] * my_gain

    for end in (0, 1):
        @pl.when(sec != end)
        def _():
            @pl.loop(0, groups)
            def _(k):
                final_copy(end, k, sec).wait_recv()

    input_grad_ref[...] = landed[...]

    @pl.when(is_end)
    def _():
        input_grad_ref[my_half, :] = nat[:, pl.ds(pl.multiple_of(sec * columns, columns), columns)]

        @pl.loop(0, groups)
        def _(k):
            @pl.loop(0, n_sec)
            def _(c):
                @pl.when(c != sec)
                def _():
                    final_copy(core, k, c).wait_send()

    @pl.when(sec >= 2)
    def _():
        @pl.loop(0, blocks)
        def _(block):
            chain_copy(block).wait_send()

    for half in (0, 1):
        for way in (0, 1):
            for hop in range(reach[way, half]):
                slot = lax.rem(me + (n_dp - hop if way == 0 else hop), n_dp)
                gather_copy(slot, half, way).wait_send()
        @pl.loop(0, n_dp)
        def _(slot):
            share_copy(core, slot, half).wait_send()

    scale_copy(core).wait_send()
    x_copy(core).wait_send()
    for kind in (0, 1):
        for n in range(per_quarter):
            lend_copy(kind, n).wait_send()
    for kind, way in streams:
        @pl.loop(0, reach[way, kind])
        def _(step):
            for half in (0, 1):
                ring_copy(kind, way, half, step).wait_send()


def solution(mesh):
    n_sec, n_dp = mesh.shape["section"], mesh.shape["dp"]

    def body(activations, norm_gain, adapter_down, adapter_up, counts, upstream):
        raw_rows, width = activations.shape[1:]
        down_t, up_t = jnp.swapaxes(adapter_down, 1, 2), jnp.swapaxes(adapter_up, 1, 2)
        rank, shard = down_t.shape[1:]
        live = upstream.shape[0]
        half_rows = live // 2
        cap = raw_rows // counts.shape[1]
        blocks = half_rows // ROWS
        packed = blocks * TILE
        span = width // QUARTERS
        wide = QUARTERS * rank
        columns = width // n_sec
        per_quarter = span // shard
        groups = half_rows // 16
        far = n_dp // 2
        dma = pltpu.SemaphoreType.DMA
        vmem = pl.BlockSpec(memory_space=pltpu.VMEM)
        hbm = pl.BlockSpec(memory_space=pl.ANY)
        input_grad, grad_down, grad_up = pl.pallas_call(
            functools.partial(kernel, n_sec, n_dp, cap),
            out_shape=(
                jax.ShapeDtypeStruct((live, columns), BF16),
                jax.ShapeDtypeStruct((1, rank, shard), F32),
                jax.ShapeDtypeStruct((1, rank, shard), F32),
            ),
            in_specs=[hbm] * 6,
            out_specs=(vmem, vmem, vmem),
            scratch_shapes=[
                pltpu.SMEM(counts.shape, jnp.int32),
                pltpu.VMEM((1, width), F32),
                pltpu.VMEM((2, rank, shard), BF16),
                pltpu.VMEM((raw_rows, width), BF16),
                pltpu.VMEM((half_rows, width), BF16),
                pltpu.VMEM((live, columns), BF16),
                pltpu.VMEM((2, n_dp, 2 * rank, shard), BF16),
                pltpu.VMEM((2, span, wide), BF16),
                pltpu.VMEM((2, wide, span), BF16),
                pltpu.VMEM((2, blocks, TILE, span), BF16),
                pltpu.VMEM((2, blocks, TILE, 128), F32),
                pltpu.VMEM((blocks, TILE, span), BF16),
                pltpu.VMEM((blocks, TILE, 128), F32),
                pltpu.VMEM((2, blocks, 8, 128), F32),
                pltpu.VMEM((2, packed, wide), BF16),
                pltpu.VMEM((2, blocks, TILE, span), BF16),
                pltpu.VMEM((blocks, TILE, span), BF16),
                pltpu.VMEM((2, blocks, TILE, wide), BF16),
                pltpu.VMEM((wide, span), F32),
                pltpu.VMEM((wide, span), F32),
                pltpu.VMEM((2, per_quarter, wide, shard), BF16),
                pltpu.VMEM((2, per_quarter, wide, shard), BF16),
                pltpu.VMEM((2, 2, 2, far + 1, rank // 2, shard), BF16),
                dma((6,)),
                dma((2, 2, n_dp)),
                dma((2, n_dp)),
                dma((2, n_dp)),
                dma((2, n_dp)),
                dma((2,)),
                dma((2,)),
                dma((blocks,)),
                dma((blocks,)),
                dma((2, per_quarter)),
                dma((2, per_quarter)),
                dma((groups, n_sec)),
                dma((2, groups)),
                dma((2, 2, 2, far + 1)),
                dma((2, 2, 2, far + 1)),
            ],
            compiler_params=pltpu.CompilerParams(
                collective_id=0, has_side_effects=True, vmem_limit_bytes=63 * 1024 * 1024
            ),
        )(counts, activations, norm_gain, down_t, up_t, upstream)
        return input_grad, jnp.swapaxes(grad_down, 1, 2), jnp.swapaxes(grad_up, 1, 2)

    return jax.shard_map(
        body,
        mesh=mesh,
        in_specs=(
            P("section", "dp", None),
            P("section", None),
            P("section", "dp", None),
            P("section", "dp", None),
            P("dp", None),
            P("dp", None),
        ),
        out_specs=(P("dp", "section"), P("section", "dp", None), P("section", "dp", None)),
        check_vma=False,
    )
```

```python
import functools

import jax
import jax.numpy as jnp
from jax import lax
from jax.experimental import pallas as pl
from jax.experimental.pallas import tpu as pltpu
from jax.sharding import PartitionSpec as P

ALPHA = 2.0
EPS = 1e-05
QUARTERS = 4
PARTS = 4
TILE = 16
ROWS = TILE // QUARTERS
MESH = pl.DeviceIdType.MESH
F32 = jnp.float32
BF16 = jnp.bfloat16


def iota(shape, dim):
    return lax.broadcasted_iota(jnp.int32, shape, dim)


def quarter_mask(shape, rank):
    quarter = (iota(shape, 0) // ROWS) % QUARTERS
    return quarter == iota(shape, 1) // rank


def dot(a, b, dims=((1,), (0,)), **kw):
    return lax.dot_general(a, b, (dims, ((), ())), preferred_element_type=F32, **kw)


def kernel(
    n_sec, n_dp, cap,
    counts_hbm, x_hbm, gain_hbm, down_hbm, up_hbm, upstream_hbm,
    input_grad_ref, grad_down_ref, grad_up_ref,
    counts_ref, gain_ref, own_maps, raw, nat, landed, pieces, weight_up, weight_down,
    held_x, row_scale, other_x, other_scale, coef_rank, projected_all,
    gin, gout, lowered_all, projected_t, part_up, part_down, lent, borrowed, slots,
    load_sem, gather_send, gather_recv, share_send, share_recv, swap_send, swap_recv,
    chain_send, chain_recv, lend_send, lend_recv, final_send, final_recv, ring_send, ring_recv,
):
    sec, me = lax.axis_index("section"), lax.axis_index("dp")
    right, left = lax.rem(me + 1, n_dp), lax.rem(me + n_dp - 1, n_dp)
    core = lax.rem(sec, 2)
    other = 1 - core
    mate = sec + 1 - 2 * core
    half_rows, width = nat.shape
    live = 2 * half_rows
    blocks = half_rows // ROWS
    packed = blocks * TILE
    span = width // QUARTERS
    rank, shard = down_hbm.shape[1:]
    per_quarter = span // shard
    columns = width // n_sec
    wide = QUARTERS * rank
    far = n_dp // 2
    is_top, is_end = sec >= n_sec - 2, sec < 2

    small = [
        pltpu.make_async_copy(up_hbm, own_maps.at[pl.ds(0, 1)], load_sem.at[2]),
        pltpu.make_async_copy(down_hbm, own_maps.at[pl.ds(1, 1)], load_sem.at[3]),
        pltpu.make_async_copy(gain_hbm, gain_ref, load_sem.at[4]),
        pltpu.make_async_copy(counts_hbm, counts_ref, load_sem.at[5]),
    ]
    for load in small:
        load.start()
    load_x = pltpu.make_async_copy(x_hbm.at[0], raw, load_sem.at[0])
    load_x.start()
    my_half = pl.ds(pl.multiple_of(core * half_rows, half_rows), half_rows)
    load_up = pltpu.make_async_copy(upstream_hbm.at[my_half], nat, load_sem.at[1])

    @pl.when(is_top)
    def _():
        load_up.start()

    barrier = pltpu.get_barrier_semaphore()

    def greet(**where):
        pl.semaphore_signal(barrier, inc=1, device_id=where, device_id_type=MESH)

    greet(dp=left)
    greet(dp=right)
    greet(section=mate)

    @pl.when(sec >= 2)
    def _():
        greet(section=sec - 2)

    @pl.when(sec < n_sec - 2)
    def _():
        greet(section=sec + 2)

    for end in (0, 1):
        @pl.when((sec >= 2) & (sec != end + 2))
        def _():
            greet(section=end)

    for load in small:
        load.wait()
    my_gain = gain_ref[:, pl.ds(pl.multiple_of(me * shard, shard), shard)]
    pieces[core, me, 0:rank, :] = own_maps[0]
    pieces[core, me, rank:2 * rank, :] = (own_maps[1].astype(F32) * my_gain).astype(BF16)

    def greeted(when, amount):
        @pl.when(when)
        def _():
            pl.semaphore_wait(barrier, amount)

    greeted(is_end, 3 + 1 + n_sec - 3)
    if n_sec > 4:
        greeted((sec >= 2) & (sec < n_sec - 2), 3 + 2)
    greeted(is_top, 3 + 1)

    cut = 2 * rank // PARTS

    def gather_copy(slot, part, way):
        span_rows = pieces.at[core, slot, pl.ds(part * cut, cut)]
        return pltpu.make_async_remote_copy(
            src_ref=span_rows,
            dst_ref=span_rows,
            send_sem=gather_send.at[way, part, slot],
            recv_sem=gather_recv.at[part, slot],
            device_id={"dp": right if way == 0 else left},
            device_id_type=MESH,
        )

    def to_mate(source, target, send_sem, recv_sem):
        return pltpu.make_async_remote_copy(
            src_ref=source,
            dst_ref=target,
            send_sem=send_sem,
            recv_sem=recv_sem,
            device_id={"section": mate},
            device_id_type=MESH,
        )

    def share_copy(parity, slot):
        piece = pieces.at[parity, slot]
        return to_mate(piece, piece, share_send.at[slot], share_recv.at[slot])

    def scale_copy(parity):
        return to_mate(other_scale, row_scale.at[parity], swap_send.at[0], swap_recv.at[0])

    def x_copy(parity):
        return to_mate(other_x, held_x.at[parity], swap_send.at[1], swap_recv.at[1])

    reach = {(0, 0): far, (0, 1): far - 1, (1, 0): far - 1, (1, 1): far}
    half_of = [2 * part // PARTS for part in range(PARTS)]
    for part in range(PARTS):
        for way in (0, 1):
            gather_copy(me, part, way).start()
    share_copy(core, me).start()

    load_x.wait()
    raw_rows = raw.shape[0]
    members = counts_ref.shape[1]

    def place(parity, slot):
        rows = pl.ds(pl.multiple_of((slot // per_quarter) * rank, rank), rank)
        cols = pl.ds(pl.multiple_of(lax.rem(slot, per_quarter) * shard, shard), shard)
        weight_down[parity, rows, cols] = pieces[parity, slot, rank:2 * rank, :]

    def sources(shape, half):
        line = iota(shape, 0)
        position = half * half_rows + (line // TILE) * ROWS + lax.rem(line, ROWS)
        source = position
        bound = jnp.int32(0)
        for member in range(members - 1):
            count = counts_ref[0, member]
            bound = bound + count
            source = source + jnp.where(position >= bound, cap - count, 0)
        return source == iota(shape, 1), (line // ROWS) % QUARTERS

    prep_rows = 16
    norm_jobs = raw_rows // prep_rows
    inverses = []

    def pack(n, half):
        chosen, quarter = sources((packed, raw_rows), half)
        total = jnp.zeros((packed, shard), F32)
        for q in range(QUARTERS):
            pick = (chosen & (quarter == q)).astype(BF16)
            total += dot(pick, raw[:, q * span + n * shard:q * span + (n + 1) * shard])
        return total.astype(BF16).reshape(blocks, TILE, shard)

    def work(job):
        if job < norm_jobs:
            rows = pl.ds(job * prep_rows, prep_rows)
            values = raw[rows, :].astype(F32)
            inverse = lax.rsqrt(jnp.mean(values * values, axis=-1, keepdims=True) + EPS)
            raw[rows, :] = (values * inverse).astype(BF16)
            inverses.append(inverse)
        elif job == norm_jobs:
            inverse_all = jnp.broadcast_to(jnp.concatenate(inverses, axis=0), (raw_rows, 128))
            for half in (other, core):
                chosen, _ = sources((packed, raw_rows), half)
                scale = dot(chosen.astype(F32), inverse_all, precision=lax.Precision.HIGHEST)
                scale = scale.reshape(blocks, TILE, 128)
                if half is other:
                    other_scale[...] = scale
                    scale_copy(core).start()
                else:
                    row_scale[core] = scale
        elif job <= norm_jobs + per_quarter:
            n = job - norm_jobs - 1
            other_x[:, :, n * shard:(n + 1) * shard] = pack(n, other)
            if n == per_quarter - 1:
                x_copy(core).start()
        elif job <= norm_jobs + 2 * per_quarter:
            n = job - norm_jobs - 1 - per_quarter
            held_x[core, :, :, n * shard:(n + 1) * shard] = pack(n, core)

    jobs = norm_jobs + 1 + 2 * per_quarter
    done = 0
    turns = PARTS * far
    turn = 0

    def from_mate(hop):
        for slot in [me] if hop == 0 else [lax.rem(me + n_dp - hop, n_dp), lax.rem(me + hop, n_dp)]:
            share_copy(other, slot).wait_recv()
            place(other, slot)
            if hop == far:
                break

    place(core, me)
    for hop in range(1, far + 1):
        for part in range(PARTS):
            for way in (0, 1):
                if hop <= reach[way, half_of[part]]:
                    slot = lax.rem(me + (n_dp - hop if way == 0 else hop), n_dp)
                    here = gather_copy(slot, part, way)
                    here.wait_recv()
                    if hop < reach[way, half_of[part]]:
                        here.start()
                    if part == PARTS - 1:
                        share_copy(core, slot).start()
                        place(core, slot)
            turn += 1
            while done * turns < jobs * turn:
                work(done)
                done += 1
        from_mate(hop - 1)

    @pl.when(is_top)
    def _():
        load_up.wait()
        line = iota((packed, half_rows), 0)
        position = (line // TILE) * ROWS + lax.rem(line, ROWS)
        chosen = position == iota((packed, half_rows), 1)
        quarter = (line // ROWS) % QUARTERS
        for n in range(per_quarter):
            cols = slice(n * shard, (n + 1) * shard)
            total = jnp.zeros((packed, shard), F32)
            for q in range(QUARTERS):
                pick = (chosen & (quarter == q)).astype(BF16)
                total += dot(pick, nat[:, q * span + n * shard:q * span + (n + 1) * shard])
            gin[1, :, :, cols] = total.astype(BF16).reshape(blocks, TILE, shard)

    from_mate(far)
    scale_copy(other).wait_recv()
    x_copy(other).wait_recv()

    for parity in (1, 0):
        for n in range(per_quarter):
            stack = [pieces[parity, q * per_quarter + n, 0:rank, :] for q in range(QUARTERS)]
            weight_up[parity, n * shard:(n + 1) * shard, :] = jnp.concatenate(stack, axis=0).T

    def fold(product):
        pair = product[:, 0:128] + product[:, 128:256]
        return pair + pltpu.roll(pair, 64, 1)

    for parity in (1, 0):
        product = dot(held_x[parity].reshape(packed, span), weight_down[parity], ((1,), (1,)))
        product = jnp.where(quarter_mask((packed, wide), rank), product, 0.0)
        folded = fold(product).reshape(blocks, TILE, 128)
        folded = folded[:, 0:8, :] + folded[:, 8:16, :]
        folded = (folded + pltpu.roll(folded, 4, 1)).astype(BF16).astype(F32)
        lane = lax.broadcasted_iota(jnp.int32, folded.shape, 2)
        coef_rank[parity] = jnp.where(lane < rank, folded * (1.0 / width), 0.0)
        tall = jnp.concatenate([folded, folded], axis=1)
        tall = jnp.concatenate([tall, tall], axis=2).reshape(packed, wide)
        projected_all[parity] = jnp.where(quarter_mask((packed, wide), rank), tall, 0.0).astype(BF16)

    def flip(values):
        return values.astype(F32).T.astype(BF16)

    late = is_top & (core == 0)

    def flip_projected():
        for parity in (0, 1):
            projected_t[parity] = flip(projected_all[parity])

    @pl.when(jnp.logical_not(late))
    def _():
        flip_projected()

    def chain_copy(block):
        return pltpu.make_async_remote_copy(
            src_ref=gout.at[block],
            dst_ref=gin.at[1, block],
            send_sem=chain_send.at[block],
            recv_sem=chain_recv.at[block],
            device_id={"section": lax.rem(sec + n_sec - 2, n_sec)},
            device_id_type=MESH,
        )

    group = 16
    group_blocks = group // ROWS
    groups = half_rows // group

    def final_copy(half, k, c):
        rows = pl.ds(pl.multiple_of(k * group, group), group)
        return pltpu.make_async_remote_copy(
            src_ref=nat.at[rows, pl.ds(pl.multiple_of(c * columns, columns), columns)],
            dst_ref=landed.at[pl.ds(pl.multiple_of(half * half_rows + k * group, group), group)],
            send_sem=final_send.at[k, c],
            recv_sem=final_recv.at[half, k],
            device_id={"section": c},
            device_id_type=MESH,
        )

    mask = quarter_mask((TILE, wide), rank)

    def spread(rows8):
        tall = jnp.concatenate([rows8, rows8], axis=0)
        tall = jnp.concatenate([tall, tall], axis=1)
        return jnp.where(mask, tall, 0.0).astype(BF16)

    def unpack(k):
        finished = gout[pl.ds(k * group_blocks, group_blocks)].reshape(group_blocks * TILE, span)
        shape = (group, group_blocks * TILE)
        row = iota(shape, 0)
        rows = pl.ds(pl.multiple_of(k * group, group), group)
        for q in range(QUARTERS):
            want = (row // ROWS) * TILE + q * ROWS + lax.rem(row, ROWS)
            pick = (want == iota(shape, 1)).astype(BF16)
            nat[rows, q * span:(q + 1) * span] = dot(pick, finished).astype(BF16)

    def hand_out(unit):
        k, late_half = unit // 2, lax.rem(unit, 2)

        @pl.when(late_half == 0)
        def _():
            unpack(k)

        @pl.loop(0, n_sec // 2)
        def _(step):
            c = late_half * (n_sec // 2) + step

            @pl.when(c != sec)
            def _():
                final_copy(core, k, c).start()

    def layer(parity, block, result):
        values = gin[parity, block]
        product = dot(values, weight_up[parity])
        pair = fold(jnp.where(mask, product, 0.0))
        pair = pair[0:8, :] + pair[8:16, :]
        lowered = ((pair + pltpu.roll(pair, 4, 0)) * ALPHA).astype(BF16).astype(F32)
        scaled = lowered * row_scale[parity, block, 0:8, :]
        coef = jnp.sum(scaled * coef_rank[parity, block], axis=-1, keepdims=True)
        coef = jnp.concatenate([coef, coef], axis=0)
        back = dot(spread(scaled), weight_down[parity])
        fresh = values.astype(F32) + (back - held_x[parity, block].astype(F32) * coef)
        result[...] = fresh.astype(BF16)
        return lowered

    def run_chain(receives, sends):
        @pl.loop(0, blocks)
        def _(block):
            if receives:
                chain_copy(block).wait_recv()
            first = layer(1, block, gin.at[0, block])
            second = layer(0, block, gout.at[block])
            if sends:
                chain_copy(block).start()
            lowered_all[1, block] = spread(first)
            lowered_all[0, block] = spread(second)

    @pl.when(is_top)
    def _():
        run_chain(False, True)

    if n_sec > 4:
        @pl.when((sec >= 2) & (sec < n_sec - 2))
        def _():
            run_chain(True, True)

    @pl.when(is_end)
    def _():
        run_chain(True, False)

    half_rank = rank // 2
    parts = (part_up, part_down)
    offsets = (0, -1, 1, 2)[:per_quarter]

    def chunk_at(offset):
        return lax.rem(me + far + per_quarter + offset, per_quarter)

    def lend_copy(kind, n):
        return to_mate(
            lent.at[kind, n], borrowed.at[kind, n], lend_send.at[kind, n], lend_recv.at[kind, n]
        )

    def products(parity, n):
        cols = pl.ds(pl.multiple_of(n * shard, shard), shard)
        up = dot(flipped[parity is core][0], gin[parity, :, :, cols].reshape(packed, shard))
        down = dot(flipped[parity is core][1], held_x[parity, :, :, cols].reshape(packed, shard))
        return cols, up * (ALPHA / live), down * (1.0 / live)

    @pl.when(late)
    def _():
        flip_projected()

    flipped = {
        parity is core: (projected_t[parity], flip(lowered_all[parity].reshape(packed, wide)))
        for parity in (other, core)
    }
    for offset in offsets:
        n = chunk_at(offset)
        _, up, down = products(other, n)
        lent[0, n] = up.astype(BF16)
        lend_copy(0, n).start()
        lent[1, n] = down.astype(BF16)
        lend_copy(1, n).start()

    def partial(offset):
        if offset not in offsets:
            return
        n = chunk_at(offset)
        cols, up, down = products(core, n)
        for kind in (0, 1):
            lend_copy(kind, n).wait_recv()
        part_up[:, cols] = up + borrowed[0, n].astype(F32)
        part_down[:, cols] = down + borrowed[1, n].astype(F32)

    def own(kind, half, piece):
        start = (piece // per_quarter) * rank + half * half_rank
        rows = pl.ds(pl.multiple_of(start, half_rank), half_rank)
        cols = pl.ds(pl.multiple_of(lax.rem(piece, per_quarter) * shard, shard), shard)
        return parts[kind][rows, cols]

    def ring_copy(kind, way, half, step):
        return pltpu.make_async_remote_copy(
            src_ref=slots.at[kind, way, half, step],
            dst_ref=slots.at[kind, way, half, step + 1],
            send_sem=ring_send.at[kind, way, half, step],
            recv_sem=ring_recv.at[kind, way, half, step + 1],
            device_id={"dp": right if way == 0 else left},
            device_id_type=MESH,
        )

    def target(kind, way, step):
        distance = reach[way, kind] - step
        return lax.rem(me + (distance if way == 0 else n_dp - distance), n_dp)

    def begin(kind, way):
        for half in (0, 1):
            slots[kind, way, half, 0] = own(kind, half, target(kind, way, 0)).astype(BF16)
            ring_copy(kind, way, half, 0).start()

    def forward(kind, way, step):
        for half in (0, 1):
            ring_copy(kind, way, half, step - 1).wait_recv()
            total = slots[kind, way, half, step].astype(F32) + own(kind, half, target(kind, way, step))
            slots[kind, way, half, step] = total.astype(BF16)
            ring_copy(kind, way, half, step).start()

    partial(0)
    begin(0, 0)
    begin(1, 1)
    partial(-1)
    begin(1, 0)
    partial(1)
    begin(0, 1)
    partial(2)
    streams = [(0, 0), (1, 1), (1, 0), (0, 1)]

    units = 2 * groups
    per_step = units // (far - 2) if far > 2 and units % (far - 2) == 0 else 0

    @pl.loop(1, far - 1)
    def _(step):
        for kind, way in streams:
            forward(kind, way, step)

        @pl.when(is_end)
        def _():
            for extra in range(per_step):
                hand_out((step - 1) * per_step + extra)

    if per_step == 0:
        @pl.when(is_end)
        def _():
            @pl.loop(0, units)
            def _(unit):
                hand_out(unit)

    for kind, way in streams[0:2]:
        forward(kind, way, far - 1)

    sums = []
    for kind in (0, 1):
        for half in (0, 1):
            total = own(kind, half, me)
            for way in (1 - kind, kind):
                ring_copy(kind, way, half, reach[way, kind] - 1).wait_recv()
                total += slots[kind, way, half, reach[way, kind]].astype(F32)
            sums.append(total)
    for half in (0, 1):
        rows = slice(half * half_rank, (half + 1) * half_rank)
        grad_up_ref[0, rows, :] = sums[half]
        grad_down_ref[0, rows, :] = sums[2 + half] * my_gain

    for end in (0, 1):
        @pl.when(sec != end)
        def _():
            @pl.loop(0, groups)
            def _(k):
                final_copy(end, k, sec).wait_recv()

    input_grad_ref[...] = landed[...]

    @pl.when(is_end)
    def _():
        input_grad_ref[my_half, :] = nat[:, pl.ds(pl.multiple_of(sec * columns, columns), columns)]

        @pl.loop(0, groups)
        def _(k):
            @pl.loop(0, n_sec)
            def _(c):
                @pl.when(c != sec)
                def _():
                    final_copy(core, k, c).wait_send()

    @pl.when(sec >= 2)
    def _():
        @pl.loop(0, blocks)
        def _(block):
            chain_copy(block).wait_send()

    for part in range(PARTS):
        for way in (0, 1):
            for hop in range(reach[way, half_of[part]]):
                slot = lax.rem(me + (n_dp - hop if way == 0 else hop), n_dp)
                gather_copy(slot, part, way).wait_send()

    @pl.loop(0, n_dp)
    def _(slot):
        share_copy(core, slot).wait_send()

    scale_copy(core).wait_send()
    x_copy(core).wait_send()
    for kind in (0, 1):
        for n in range(per_quarter):
            lend_copy(kind, n).wait_send()
    for kind, way in streams:
        @pl.loop(0, reach[way, kind])
        def _(step):
            for half in (0, 1):
                ring_copy(kind, way, half, step).wait_send()


def solution(mesh):
    n_sec, n_dp = mesh.shape["section"], mesh.shape["dp"]

    def body(activations, norm_gain, adapter_down, adapter_up, counts, upstream):
        raw_rows, width = activations.shape[1:]
        down_t, up_t = jnp.swapaxes(adapter_down, 1, 2), jnp.swapaxes(adapter_up, 1, 2)
        rank, shard = down_t.shape[1:]
        live = upstream.shape[0]
        half_rows = live // 2
        cap = raw_rows // counts.shape[1]
        blocks = half_rows // ROWS
        packed = blocks * TILE
        span = width // QUARTERS
        wide = QUARTERS * rank
        columns = width // n_sec
        per_quarter = span // shard
        groups = half_rows // 16
        far = n_dp // 2
        dma = pltpu.SemaphoreType.DMA
        vmem = pl.BlockSpec(memory_space=pltpu.VMEM)
        hbm = pl.BlockSpec(memory_space=pl.ANY)
        input_grad, grad_down, grad_up = pl.pallas_call(
            functools.partial(kernel, n_sec, n_dp, cap),
            out_shape=(
                jax.ShapeDtypeStruct((live, columns), BF16),
                jax.ShapeDtypeStruct((1, rank, shard), F32),
                jax.ShapeDtypeStruct((1, rank, shard), F32),
            ),
            in_specs=[hbm] * 6,
            out_specs=(vmem, vmem, vmem),
            scratch_shapes=[
                pltpu.SMEM(counts.shape, jnp.int32),
                pltpu.VMEM((1, width), F32),
                pltpu.VMEM((2, rank, shard), BF16),
                pltpu.VMEM((raw_rows, width), BF16),
                pltpu.VMEM((half_rows, width), BF16),
                pltpu.VMEM((live, columns), BF16),
                pltpu.VMEM((2, n_dp, 2 * rank, shard), BF16),
                pltpu.VMEM((2, span, wide), BF16),
                pltpu.VMEM((2, wide, span), BF16),
                pltpu.VMEM((2, blocks, TILE, span), BF16),
                pltpu.VMEM((2, blocks, TILE, 128), F32),
                pltpu.VMEM((blocks, TILE, span), BF16),
                pltpu.VMEM((blocks, TILE, 128), F32),
                pltpu.VMEM((2, blocks, 8, 128), F32),
                pltpu.VMEM((2, packed, wide), BF16),
                pltpu.VMEM((2, blocks, TILE, span), BF16),
                pltpu.VMEM((blocks, TILE, span), BF16),
                pltpu.VMEM((2, blocks, TILE, wide), BF16),
                pltpu.VMEM((2, wide, packed), BF16),
                pltpu.VMEM((wide, span), F32),
                pltpu.VMEM((wide, span), F32),
                pltpu.VMEM((2, per_quarter, wide, shard), BF16),
                pltpu.VMEM((2, per_quarter, wide, shard), BF16),
                pltpu.VMEM((2, 2, 2, far + 1, rank // 2, shard), BF16),
                dma((6,)),
                dma((2, PARTS, n_dp)),
                dma((PARTS, n_dp)),
                dma((n_dp,)),
                dma((n_dp,)),
                dma((2,)),
                dma((2,)),
                dma((blocks,)),
                dma((blocks,)),
                dma((2, per_quarter)),
                dma((2, per_quarter)),
                dma((groups, n_sec)),
                dma((2, groups)),
                dma((2, 2, 2, far + 1)),
                dma((2, 2, 2, far + 1)),
            ],
            compiler_params=pltpu.CompilerParams(
                collective_id=0, has_side_effects=True, vmem_limit_bytes=63 * 1024 * 1024
            ),
        )(counts, activations, norm_gain, down_t, up_t, upstream)
        return input_grad, jnp.swapaxes(grad_down, 1, 2), jnp.swapaxes(grad_up, 1, 2)

    return jax.shard_map(
        body,
        mesh=mesh,
        in_specs=(
            P("section", "dp", None),
            P("section", None),
            P("section", "dp", None),
            P("section", "dp", None),
            P("dp", None),
            P("dp", None),
        ),
        out_specs=(P("dp", "section"), P("section", "dp", None), P("section", "dp", None)),
        check_vma=False,
    )
```

```python
import functools

import jax
import jax.numpy as jnp
from jax import lax
from jax.experimental import pallas as pl
from jax.experimental.pallas import tpu as pltpu
from jax.sharding import PartitionSpec as P

ALPHA = 2.0
EPS = 1e-05
QUARTERS = 4
PARTS = 4
TILE = 16
ROWS = TILE // QUARTERS
MESH = pl.DeviceIdType.MESH
F32 = jnp.float32
BF16 = jnp.bfloat16


def iota(shape, dim):
    return lax.broadcasted_iota(jnp.int32, shape, dim)


def quarter_mask(shape, rank):
    quarter = (iota(shape, 0) // ROWS) % QUARTERS
    return quarter == iota(shape, 1) // rank


def dot(a, b, dims=((1,), (0,)), **kw):
    return lax.dot_general(a, b, (dims, ((), ())), preferred_element_type=F32, **kw)


def kernel(
    n_sec, n_dp, cap,
    counts_hbm, x_hbm, gain_hbm, down_hbm, up_hbm, upstream_hbm,
    input_grad_ref, grads_ref,
    counts_ref, gain_ref, own_maps, raw, nat, landed, pieces, weight_up, weight_down,
    held_x, row_scale, other_x, other_scale, coef_rank, projected_all,
    gin, gout, lowered_all, projected_t, part_up, part_down, lent, borrowed, slots,
    load_sem, gather_send, gather_recv, share_send, share_recv, swap_send, swap_recv,
    chain_send, chain_recv, lend_send, lend_recv, final_send, final_recv, ring_send, ring_recv,
):
    sec, me = lax.axis_index("section"), lax.axis_index("dp")
    right, left = lax.rem(me + 1, n_dp), lax.rem(me + n_dp - 1, n_dp)
    core = lax.rem(sec, 2)
    other = 1 - core
    mate = sec + 1 - 2 * core
    half_rows, width = nat.shape
    live = 2 * half_rows
    blocks = half_rows // ROWS
    packed = blocks * TILE
    span = width // QUARTERS
    rank, shard = down_hbm.shape[1:]
    per_quarter = span // shard
    columns = width // n_sec
    wide = QUARTERS * rank
    far = n_dp // 2
    is_top, is_end = sec >= n_sec - 2, sec < 2

    small = [
        pltpu.make_async_copy(up_hbm, own_maps.at[pl.ds(0, 1)], load_sem.at[2]),
        pltpu.make_async_copy(down_hbm, own_maps.at[pl.ds(1, 1)], load_sem.at[3]),
        pltpu.make_async_copy(gain_hbm, gain_ref, load_sem.at[4]),
        pltpu.make_async_copy(counts_hbm, counts_ref, load_sem.at[5]),
    ]
    for load in small:
        load.start()
    load_x = pltpu.make_async_copy(x_hbm.at[0], raw, load_sem.at[0])
    load_x.start()
    my_half = pl.ds(pl.multiple_of(core * half_rows, half_rows), half_rows)
    load_up = pltpu.make_async_copy(upstream_hbm.at[my_half], nat, load_sem.at[1])

    @pl.when(is_top)
    def _():
        load_up.start()

    barrier = pltpu.get_barrier_semaphore()

    def greet(**where):
        pl.semaphore_signal(barrier, inc=1, device_id=where, device_id_type=MESH)

    greet(dp=left)
    greet(dp=right)
    greet(section=mate)

    @pl.when(sec >= 2)
    def _():
        greet(section=sec - 2)

    @pl.when(sec < n_sec - 2)
    def _():
        greet(section=sec + 2)

    for end in (0, 1):
        @pl.when((sec >= 2) & (sec != end + 2))
        def _():
            greet(section=end)

    for load in small:
        load.wait()
    my_gain = gain_ref[:, pl.ds(pl.multiple_of(me * shard, shard), shard)]
    pieces[core, me, 0:rank, :] = own_maps[0]
    pieces[core, me, rank:2 * rank, :] = (own_maps[1].astype(F32) * my_gain).astype(BF16)

    def greeted(when, amount):
        @pl.when(when)
        def _():
            pl.semaphore_wait(barrier, amount)

    greeted(is_end, 3 + 1 + n_sec - 3)
    if n_sec > 4:
        greeted((sec >= 2) & (sec < n_sec - 2), 3 + 2)
    greeted(is_top, 3 + 1)

    cut = 2 * rank // PARTS

    def gather_copy(slot, part, way):
        span_rows = pieces.at[core, slot, pl.ds(part * cut, cut)]
        return pltpu.make_async_remote_copy(
            src_ref=span_rows,
            dst_ref=span_rows,
            send_sem=gather_send.at[way, part, slot],
            recv_sem=gather_recv.at[part, slot],
            device_id={"dp": right if way == 0 else left},
            device_id_type=MESH,
        )

    def to_mate(source, target, send_sem, recv_sem):
        return pltpu.make_async_remote_copy(
            src_ref=source,
            dst_ref=target,
            send_sem=send_sem,
            recv_sem=recv_sem,
            device_id={"section": mate},
            device_id_type=MESH,
        )

    def share_copy(parity, slot):
        piece = pieces.at[parity, slot]
        return to_mate(piece, piece, share_send.at[slot], share_recv.at[slot])

    def scale_copy(parity):
        return to_mate(other_scale, row_scale.at[parity], swap_send.at[0], swap_recv.at[0])

    def x_copy(parity):
        return to_mate(other_x, held_x.at[parity], swap_send.at[1], swap_recv.at[1])

    reach = {(0, 0): far, (0, 1): far - 1, (1, 0): far - 1, (1, 1): far}
    half_of = [2 * part // PARTS for part in range(PARTS)]
    for part in range(PARTS):
        for way in (0, 1):
            gather_copy(me, part, way).start()
    share_copy(core, me).start()

    load_x.wait()
    raw_rows = raw.shape[0]
    members = counts_ref.shape[1]

    def place(parity, slot):
        rows = pl.ds(pl.multiple_of((slot // per_quarter) * rank, rank), rank)
        cols = pl.ds(pl.multiple_of(lax.rem(slot, per_quarter) * shard, shard), shard)
        weight_down[parity, rows, cols] = pieces[parity, slot, rank:2 * rank, :]

    def sources(shape, half):
        line = iota(shape, 0)
        position = half * half_rows + (line // TILE) * ROWS + lax.rem(line, ROWS)
        source = position
        bound = jnp.int32(0)
        for member in range(members - 1):
            count = counts_ref[0, member]
            bound = bound + count
            source = source + jnp.where(position >= bound, cap - count, 0)
        return source == iota(shape, 1), (line // ROWS) % QUARTERS

    prep_rows = 16
    norm_jobs = raw_rows // prep_rows
    inverses = []

    def pack(n, half):
        chosen, quarter = sources((packed, raw_rows), half)
        total = jnp.zeros((packed, shard), F32)
        for q in range(QUARTERS):
            pick = (chosen & (quarter == q)).astype(BF16)
            total += dot(pick, raw[:, q * span + n * shard:q * span + (n + 1) * shard])
        return total.astype(BF16).reshape(blocks, TILE, shard)

    def work(job):
        if job < norm_jobs:
            rows = pl.ds(job * prep_rows, prep_rows)
            values = raw[rows, :].astype(F32)
            inverse = lax.rsqrt(jnp.mean(values * values, axis=-1, keepdims=True) + EPS)
            raw[rows, :] = (values * inverse).astype(BF16)
            inverses.append(inverse)
        elif job == norm_jobs:
            inverse_all = jnp.broadcast_to(jnp.concatenate(inverses, axis=0), (raw_rows, 128))
            for half in (other, core):
                chosen, _ = sources((packed, raw_rows), half)
                scale = dot(chosen.astype(F32), inverse_all, precision=lax.Precision.HIGHEST)
                scale = scale.reshape(blocks, TILE, 128)
                if half is other:
                    other_scale[...] = scale
                    scale_copy(core).start()
                else:
                    row_scale[core] = scale
        elif job <= norm_jobs + per_quarter:
            n = job - norm_jobs - 1
            other_x[:, :, n * shard:(n + 1) * shard] = pack(n, other)
            if n == per_quarter - 1:
                x_copy(core).start()
        elif job <= norm_jobs + 2 * per_quarter:
            n = job - norm_jobs - 1 - per_quarter
            held_x[core, :, :, n * shard:(n + 1) * shard] = pack(n, core)

    jobs = norm_jobs + 1 + 2 * per_quarter
    done = 0
    turns = PARTS * far
    turn = 0

    def from_mate(hop):
        for slot in [me] if hop == 0 else [lax.rem(me + n_dp - hop, n_dp), lax.rem(me + hop, n_dp)]:
            share_copy(other, slot).wait_recv()
            place(other, slot)
            if hop == far:
                break

    place(core, me)
    for hop in range(1, far + 1):
        for part in range(PARTS):
            for way in (0, 1):
                if hop <= reach[way, half_of[part]]:
                    slot = lax.rem(me + (n_dp - hop if way == 0 else hop), n_dp)
                    here = gather_copy(slot, part, way)
                    here.wait_recv()
                    if hop < reach[way, half_of[part]]:
                        here.start()
                    if part == PARTS - 1:
                        share_copy(core, slot).start()
                        place(core, slot)
            turn += 1
            while done * turns < jobs * turn:
                work(done)
                done += 1
        from_mate(hop - 1)

    @pl.when(is_top)
    def _():
        load_up.wait()
        line = iota((packed, half_rows), 0)
        position = (line // TILE) * ROWS + lax.rem(line, ROWS)
        chosen = position == iota((packed, half_rows), 1)
        quarter = (line // ROWS) % QUARTERS
        for n in range(per_quarter):
            cols = slice(n * shard, (n + 1) * shard)
            total = jnp.zeros((packed, shard), F32)
            for q in range(QUARTERS):
                pick = (chosen & (quarter == q)).astype(BF16)
                total += dot(pick, nat[:, q * span + n * shard:q * span + (n + 1) * shard])
            gin[1, :, :, cols] = total.astype(BF16).reshape(blocks, TILE, shard)

    from_mate(far)
    scale_copy(other).wait_recv()
    x_copy(other).wait_recv()

    for parity in (1, 0):
        for n in range(per_quarter):
            stack = [pieces[parity, q * per_quarter + n, 0:rank, :] for q in range(QUARTERS)]
            weight_up[parity, n * shard:(n + 1) * shard, :] = jnp.concatenate(stack, axis=0).T

    def fold(product):
        pair = product[:, 0:128] + product[:, 128:256]
        return pair + pltpu.roll(pair, 64, 1)

    for parity in (1, 0):
        product = dot(held_x[parity].reshape(packed, span), weight_down[parity], ((1,), (1,)))
        product = jnp.where(quarter_mask((packed, wide), rank), product, 0.0)
        folded = fold(product).reshape(blocks, TILE, 128)
        folded = folded[:, 0:8, :] + folded[:, 8:16, :]
        folded = (folded + pltpu.roll(folded, 4, 1)).astype(BF16).astype(F32)
        lane = lax.broadcasted_iota(jnp.int32, folded.shape, 2)
        coef_rank[parity] = jnp.where(lane < rank, folded * (1.0 / width), 0.0)
        tall = jnp.concatenate([folded, folded], axis=1)
        tall = jnp.concatenate([tall, tall], axis=2).reshape(packed, wide)
        projected_all[parity] = jnp.where(quarter_mask((packed, wide), rank), tall, 0.0).astype(BF16)

    def flip(values):
        return values.astype(F32).T.astype(BF16)

    late = is_top & (core == 0)

    def flip_projected():
        for parity in (0, 1):
            projected_t[parity] = flip(projected_all[parity])

    @pl.when(jnp.logical_not(late))
    def _():
        flip_projected()

    def chain_copy(block, side):
        cols = pl.ds(side * (span // 2), span // 2)
        return pltpu.make_async_remote_copy(
            src_ref=gout.at[block, :, cols],
            dst_ref=gin.at[1, block, :, cols],
            send_sem=chain_send.at[block, side],
            recv_sem=chain_recv.at[block, side],
            device_id={"section": lax.rem(sec + n_sec - 2, n_sec)},
            device_id_type=MESH,
        )

    group = 16
    group_blocks = group // ROWS
    groups = half_rows // group

    def final_copy(half, k, c):
        rows = pl.ds(pl.multiple_of(k * group, group), group)
        return pltpu.make_async_remote_copy(
            src_ref=nat.at[rows, pl.ds(pl.multiple_of(c * columns, columns), columns)],
            dst_ref=landed.at[pl.ds(pl.multiple_of(half * half_rows + k * group, group), group)],
            send_sem=final_send.at[k, c],
            recv_sem=final_recv.at[half, k],
            device_id={"section": c},
            device_id_type=MESH,
        )

    mask = quarter_mask((TILE, wide), rank)

    def spread(rows8):
        tall = jnp.concatenate([rows8, rows8], axis=0)
        tall = jnp.concatenate([tall, tall], axis=1)
        return jnp.where(mask, tall, 0.0).astype(BF16)

    def unpack(k):
        finished = gout[pl.ds(k * group_blocks, group_blocks)].reshape(group_blocks * TILE, span)
        shape = (group, group_blocks * TILE)
        row = iota(shape, 0)
        rows = pl.ds(pl.multiple_of(k * group, group), group)
        for q in range(QUARTERS):
            want = (row // ROWS) * TILE + q * ROWS + lax.rem(row, ROWS)
            pick = (want == iota(shape, 1)).astype(BF16)
            nat[rows, q * span:(q + 1) * span] = dot(pick, finished).astype(BF16)

    def hand_out(unit):
        k, late_half = unit // 2, lax.rem(unit, 2)

        @pl.when(late_half == 0)
        def _():
            unpack(k)

        @pl.loop(0, n_sec // 2)
        def _(step):
            c = late_half * (n_sec // 2) + step

            @pl.when(c != sec)
            def _():
                final_copy(core, k, c).start()

    def layer(parity, block, result, sends):
        values = gin[parity, block]
        product = dot(values, weight_up[parity])
        pair = fold(jnp.where(mask, product, 0.0))
        pair = pair[0:8, :] + pair[8:16, :]
        lowered = ((pair + pltpu.roll(pair, 4, 0)) * ALPHA).astype(BF16).astype(F32)
        scaled = lowered * row_scale[parity, block, 0:8, :]
        coef = jnp.sum(scaled * coef_rank[parity, block], axis=-1, keepdims=True)
        coef = jnp.concatenate([coef, coef], axis=0)
        scaled = spread(scaled)
        for side in (0, 1):
            cols = slice(side * (span // 2), (side + 1) * (span // 2))
            back = dot(scaled, weight_down[parity, :, cols])
            fresh = values[:, cols].astype(F32) + (back - held_x[parity, block, :, cols].astype(F32) * coef)
            result[:, cols] = fresh.astype(BF16)
            if sends:
                chain_copy(block, side).start()
        return lowered

    def run_chain(receives, sends):
        @pl.loop(0, blocks)
        def _(block):
            if receives:
                for side in (0, 1):
                    chain_copy(block, side).wait_recv()
            first = layer(1, block, gin.at[0, block], False)
            second = layer(0, block, gout.at[block], sends)
            lowered_all[1, block] = spread(first)
            lowered_all[0, block] = spread(second)

    @pl.when(is_top)
    def _():
        run_chain(False, True)

    if n_sec > 4:
        @pl.when((sec >= 2) & (sec < n_sec - 2))
        def _():
            run_chain(True, True)

    @pl.when(is_end)
    def _():
        run_chain(True, False)

    half_rank = rank // 2
    parts = (part_up, part_down)
    offsets = (0, -1, 1, 2)[:per_quarter]

    def chunk_at(offset):
        return lax.rem(me + far + per_quarter + offset, per_quarter)

    def lend_copy(kind, n):
        return to_mate(
            lent.at[kind, n], borrowed.at[kind, n], lend_send.at[kind, n], lend_recv.at[kind, n]
        )

    def products(parity, n):
        cols = pl.ds(pl.multiple_of(n * shard, shard), shard)
        up = dot(flipped[parity is core][0], gin[parity, :, :, cols].reshape(packed, shard))
        down = dot(flipped[parity is core][1], held_x[parity, :, :, cols].reshape(packed, shard))
        return cols, up, down

    @pl.when(late)
    def _():
        flip_projected()

    flipped = {
        parity is core: (projected_t[parity], flip(lowered_all[parity].reshape(packed, wide)))
        for parity in (other, core)
    }
    for offset in offsets:
        n = chunk_at(offset)
        _, up, down = products(other, n)
        lent[0, n] = up.astype(BF16)
        lend_copy(0, n).start()
        lent[1, n] = down.astype(BF16)
        lend_copy(1, n).start()

    def partial(offset):
        if offset not in offsets:
            return
        n = chunk_at(offset)
        cols, up, down = products(core, n)
        for kind in (0, 1):
            lend_copy(kind, n).wait_recv()
        part_up[:, cols] = up + borrowed[0, n].astype(F32)
        part_down[:, cols] = down + borrowed[1, n].astype(F32)

    def own(kind, half, piece):
        start = (piece // per_quarter) * rank + half * half_rank
        rows = pl.ds(pl.multiple_of(start, half_rank), half_rank)
        cols = pl.ds(pl.multiple_of(lax.rem(piece, per_quarter) * shard, shard), shard)
        return parts[kind][rows, cols]

    def ring_copy(kind, way, half, step):
        return pltpu.make_async_remote_copy(
            src_ref=slots.at[kind, way, half, step],
            dst_ref=slots.at[kind, way, half, step + 1],
            send_sem=ring_send.at[kind, way, half, step],
            recv_sem=ring_recv.at[kind, way, half, step + 1],
            device_id={"dp": right if way == 0 else left},
            device_id_type=MESH,
        )

    def target(kind, way, step):
        distance = reach[way, kind] - step
        return lax.rem(me + (distance if way == 0 else n_dp - distance), n_dp)

    def begin(kind, way):
        for half in (0, 1):
            slots[kind, way, half, 0] = own(kind, half, target(kind, way, 0)).astype(BF16)
            ring_copy(kind, way, half, 0).start()

    def forward(kind, way, step):
        for half in (0, 1):
            ring_copy(kind, way, half, step - 1).wait_recv()
            total = slots[kind, way, half, step].astype(F32) + own(kind, half, target(kind, way, step))
            slots[kind, way, half, step] = total.astype(BF16)
            ring_copy(kind, way, half, step).start()

    partial(0)
    begin(0, 0)
    begin(1, 1)
    partial(-1)
    begin(1, 0)
    partial(1)
    begin(0, 1)
    partial(2)
    streams = [(0, 0), (1, 1), (1, 0), (0, 1)]

    units = 2 * groups
    per_step = units // (far - 2) if far > 2 and units % (far - 2) == 0 else 0

    @pl.loop(1, far - 1)
    def _(step):
        for kind, way in streams:
            forward(kind, way, step)

        @pl.when(is_end)
        def _():
            for extra in range(per_step):
                hand_out((step - 1) * per_step + extra)

    if per_step == 0:
        @pl.when(is_end)
        def _():
            @pl.loop(0, units)
            def _(unit):
                hand_out(unit)

    for kind, way in streams[0:2]:
        forward(kind, way, far - 1)

    sums = []
    for kind in (0, 1):
        for half in (0, 1):
            total = own(kind, half, me)
            for way in (1 - kind, kind):
                ring_copy(kind, way, half, reach[way, kind] - 1).wait_recv()
                total += slots[kind, way, half, reach[way, kind]].astype(F32)
            sums.append(total)
    for half in (0, 1):
        rows = slice(half * half_rank, (half + 1) * half_rank)
        grads_ref[0, rows, :] = sums[half]
        grads_ref[1, rows, :] = sums[2 + half] * my_gain

    for end in (0, 1):
        @pl.when(sec != end)
        def _():
            @pl.loop(0, groups)
            def _(k):
                final_copy(end, k, sec).wait_recv()

    input_grad_ref[...] = landed[...]

    @pl.when(is_end)
    def _():
        input_grad_ref[my_half, :] = nat[:, pl.ds(pl.multiple_of(sec * columns, columns), columns)]

        @pl.loop(0, groups)
        def _(k):
            @pl.loop(0, n_sec)
            def _(c):
                @pl.when(c != sec)
                def _():
                    final_copy(core, k, c).wait_send()

    @pl.when(sec >= 2)
    def _():
        @pl.loop(0, blocks)
        def _(block):
            for side in (0, 1):
                chain_copy(block, side).wait_send()

    for part in range(PARTS):
        for way in (0, 1):
            for hop in range(reach[way, half_of[part]]):
                slot = lax.rem(me + (n_dp - hop if way == 0 else hop), n_dp)
                gather_copy(slot, part, way).wait_send()

    @pl.loop(0, n_dp)
    def _(slot):
        share_copy(core, slot).wait_send()

    scale_copy(core).wait_send()
    x_copy(core).wait_send()
    for kind in (0, 1):
        for n in range(per_quarter):
            lend_copy(kind, n).wait_send()
    for kind, way in streams:
        @pl.loop(0, reach[way, kind])
        def _(step):
            for half in (0, 1):
                ring_copy(kind, way, half, step).wait_send()


def solution(mesh):
    n_sec, n_dp = mesh.shape["section"], mesh.shape["dp"]

    def body(activations, norm_gain, adapter_down, adapter_up, counts, upstream):
        raw_rows, width = activations.shape[1:]
        down_t, up_t = jnp.swapaxes(adapter_down, 1, 2), jnp.swapaxes(adapter_up, 1, 2)
        rank, shard = down_t.shape[1:]
        live = upstream.shape[0]
        half_rows = live // 2
        cap = raw_rows // counts.shape[1]
        blocks = half_rows // ROWS
        packed = blocks * TILE
        span = width // QUARTERS
        wide = QUARTERS * rank
        columns = width // n_sec
        per_quarter = span // shard
        groups = half_rows // 16
        far = n_dp // 2
        dma = pltpu.SemaphoreType.DMA
        vmem = pl.BlockSpec(memory_space=pltpu.VMEM)
        hbm = pl.BlockSpec(memory_space=pl.ANY)
        input_grad, grads = pl.pallas_call(
            functools.partial(kernel, n_sec, n_dp, cap),
            out_shape=(
                jax.ShapeDtypeStruct((live, columns), BF16),
                jax.ShapeDtypeStruct((2, rank, shard), F32),
            ),
            in_specs=[hbm] * 6,
            out_specs=(vmem, vmem),
            scratch_shapes=[
                pltpu.SMEM(counts.shape, jnp.int32),
                pltpu.VMEM((1, width), F32),
                pltpu.VMEM((2, rank, shard), BF16),
                pltpu.VMEM((raw_rows, width), BF16),
                pltpu.VMEM((half_rows, width), BF16),
                pltpu.VMEM((live, columns), BF16),
                pltpu.VMEM((2, n_dp, 2 * rank, shard), BF16),
                pltpu.VMEM((2, span, wide), BF16),
                pltpu.VMEM((2, wide, span), BF16),
                pltpu.VMEM((2, blocks, TILE, span), BF16),
                pltpu.VMEM((2, blocks, TILE, 128), F32),
                pltpu.VMEM((blocks, TILE, span), BF16),
                pltpu.VMEM((blocks, TILE, 128), F32),
                pltpu.VMEM((2, blocks, 8, 128), F32),
                pltpu.VMEM((2, packed, wide), BF16),
                pltpu.VMEM((2, blocks, TILE, span), BF16),
                pltpu.VMEM((blocks, TILE, span), BF16),
                pltpu.VMEM((2, blocks, TILE, wide), BF16),
                pltpu.VMEM((2, wide, packed), BF16),
                pltpu.VMEM((wide, span), F32),
                pltpu.VMEM((wide, span), F32),
                pltpu.VMEM((2, per_quarter, wide, shard), BF16),
                pltpu.VMEM((2, per_quarter, wide, shard), BF16),
                pltpu.VMEM((2, 2, 2, far + 1, rank // 2, shard), BF16),
                dma((6,)),
                dma((2, PARTS, n_dp)),
                dma((PARTS, n_dp)),
                dma((n_dp,)),
                dma((n_dp,)),
                dma((2,)),
                dma((2,)),
                dma((blocks, 2)),
                dma((blocks, 2)),
                dma((2, per_quarter)),
                dma((2, per_quarter)),
                dma((groups, n_sec)),
                dma((2, groups)),
                dma((2, 2, 2, far + 1)),
                dma((2, 2, 2, far + 1)),
            ],
            compiler_params=pltpu.CompilerParams(
                collective_id=0, has_side_effects=True, vmem_limit_bytes=63 * 1024 * 1024
            ),
        )(counts, activations, norm_gain, down_t, up_t, upstream)
        grads = jnp.swapaxes(grads, 1, 2)
        return input_grad, grads[1:2] * (1.0 / live), grads[0:1] * (ALPHA / live)

    return jax.shard_map(
        body,
        mesh=mesh,
        in_specs=(
            P("section", "dp", None),
            P("section", None),
            P("section", "dp", None),
            P("section", "dp", None),
            P("dp", None),
            P("dp", None),
        ),
        out_specs=(P("dp", "section"), P("section", "dp", None), P("section", "dp", None)),
        check_vma=False,
    )
```
